512 devices in a mesh: dp: 32 (over z_lo, x, core), fsdp: 16 (over z_hi, y).
Axes of the slice: x: 4, y: 4, z: 16 (z_hi: 4, z_lo: 4; z = z_hi * 4 + z_lo), core: 2. Of those that a mesh axis runs over, the one named last changes fastest.
Arguments:
- grad_partials: bfloat16 [32, 16, 2, 64, 5120], P('dp', 'fsdp'), may hold values from -5 to 5
- momentum: float32 [32, 2, 64, 5120], P('dp', None, 'fsdp'), may hold values from -6 to 6
- params: float32 [2, 64, 5120], P(None, 'fsdp'), may hold values from -6 to 6
- kept: int32 [8], replicated, may hold values from 0 to 63, as said below
Outputs:
- new_params: float32 [2, 64, 5120], P(None, 'fsdp')
- new_momentum: float32 [32, 2, 64, 5120], P('dp', None, 'fsdp')
The draws below stay inside these ranges and needn't reach their ends.
Inputs may be any that keep to these rules, and one draw needn't show every extreme that they name: `kept`: 8 distinct coefficient indices.
All inputs are finite; a program needn't handle non-finite values.
Results may differ from the reference program's by a relative error of at most 0.0003.
Values sent between devices are 32-bit elements; how exact they have to be, the bound alone decides.
No kernel may reach another device: no remote copies, remote signals or barrier semaphores. Data moves between devices by JAX's collectives and lax.ppermute only.
A program may use at most 64 MiB of HBM per device.

```python
import jax
import jax.numpy as jnp
from jax import lax

SPAN = 64
KEEP = 8
ROW_VALS = 5120
LAYERS = 2
ROWS = 64
N_DP = 32
N_FSDP = 16


def draw_kept(key, part):
    key = jax.random.fold_in(key, 7)
    inner_key = jax.random.fold_in(key, 1)
    order_key = jax.random.fold_in(key, 2)
    inner = jax.random.permutation(inner_key, SPAN - 2)[:KEEP - 2].astype(jnp.int32) + 1
    ends = jnp.array([0, SPAN - 1], dtype=jnp.int32)
    joined = jnp.concatenate([ends, inner])
    return jax.random.permutation(order_key, joined).astype(jnp.int32)


def raised(values, own_key, source, target, blocks, factor):
    def block_of(dim):
        return (jnp.arange(values.shape[dim]) // (values.shape[dim] // blocks)).reshape((-1,) + (1,) * (values.ndim - 1 - dim))

    near = jax.random.permutation(own_key, blocks)[block_of(target)]
    second = (block_of(target) + blocks // 2) % blocks
    return jnp.where((block_of(source) == near) | (block_of(source) == second), factor * values, values)


def shard_levels(own_key, dims, pieces, least, high):
    def one(axis_at, blocks):
        steps = jax.random.uniform(jax.random.fold_in(jax.random.fold_in(own_key, 6), axis_at), (blocks,), jnp.float32, least / len(pieces), high / len(pieces))
        return jnp.repeat(jnp.exp(steps), dims[axis_at] // blocks).reshape((-1,) + (1,) * (len(dims) - axis_at - 1))

    factor_of = one(*pieces[0])
    for cut in pieces[1:]:
        factor_of = factor_of * one(*cut)
    return factor_of


def gaussian(own_key, dims, scale, bound, cuts=(), kind=jnp.bfloat16):
    result = jax.random.normal(own_key, dims, jnp.float32) * scale
    if len(cuts) > 0:
        result = shard_levels(own_key, dims, cuts, -0.22, 0.18) * result
    return jnp.clip(result, min=-bound, max=bound).astype(kind)


def noise_with(key, extent, deviation, most, split, heavy, kind=jnp.bfloat16):
    values = deviation * jax.random.normal(key, extent, jnp.float32)
    if split:
        values = values * shard_levels(key, extent, split, -0.22, 0.18)
    return jnp.clip(raised(values, jax.random.fold_in(key, 3), *heavy), -most, most).astype(kind)


def setup_inputs(seed: int = 0) -> dict:
    key_list = jax.random.split(jax.random.key(seed), 5)
    grad_partials = noise_with(key_list[0], (N_DP, N_FSDP, LAYERS, ROWS, ROW_VALS), 0.25, 5.0, ((0, 32), (1, 16)), (1, 3, 16, 2.0))
    momentum = gaussian(key_list[1], (N_DP, LAYERS, ROWS, ROW_VALS), 1.0, 6.0, ((0, 32), (2, 16)), jnp.float32)
    params = gaussian(key_list[2], (LAYERS, ROWS, ROW_VALS), 1.0, 6.0, ((1, 16),), jnp.float32)
    kept = draw_kept(jax.random.fold_in(key_list[4], 71), 0)
    return {"grad_partials": grad_partials, "momentum": momentum, "params": params, "kept": kept}


def dct_table():
    k = lax.broadcasted_iota(jnp.float32, (SPAN, SPAN), 0)
    n = lax.broadcasted_iota(jnp.float32, (SPAN, SPAN), 1)
    scale = jnp.where(k == 0, jnp.sqrt(1.0 / SPAN), jnp.sqrt(2.0 / SPAN))
    return scale * jnp.cos(jnp.pi * (2.0 * n + 1.0) * k / (2.0 * SPAN))

def picked_rows(kept):
    onehot = (kept[:, None] == jnp.arange(SPAN, dtype=jnp.int32)[None, :]).astype(jnp.float32)
    return jnp.dot(onehot, dct_table(), precision=lax.Precision.HIGHEST)

def reference(grad_partials, momentum, params, kept):
    picked = picked_rows(kept)
    blocks = ROW_VALS // SPAN

    def one_replica(pair):
        parts, state = pair
        grad = lax.optimization_barrier(jnp.sum(parts.astype(jnp.float32), axis=0))
        moment = 0.9 * state + grad
        spans = moment.reshape(LAYERS, ROWS, blocks, SPAN)
        coeffs = jnp.einsum('lrcn,jn->lrcj', spans, picked, precision=lax.Precision.HIGHEST)
        local = jnp.einsum('lrcj,jn->lrcn', coeffs, picked, precision=lax.Precision.HIGHEST)
        return (moment - local.reshape(moment.shape), coeffs.reshape(LAYERS, ROWS, blocks * KEEP))
    new_momentum, coeffs = lax.map(one_replica, (grad_partials, momentum))
    shared = lax.optimization_barrier(jnp.sum(coeffs, axis=0)) / N_DP
    update = jnp.einsum('lrcj,jn->lrcn', shared.reshape(LAYERS, ROWS, blocks, KEEP), picked, precision=lax.Precision.HIGHEST)
    new_params = params - update.reshape(params.shape)
    return (new_params, new_momentum)
```

```python
import functools

import jax
import jax.numpy as jnp
import numpy as np
from jax import lax
from jax.experimental import pallas as pl
from jax.experimental.pallas import tpu as pltpu
from jax.sharding import PartitionSpec as P

SPAN = 64
KEEP = 8
ROW_VALS = 5120
LAYERS = 2
GROUP = 128 // KEEP
WIDE = GROUP * SPAN
CHUNKS = ROW_VALS // WIDE
COEFFS = ROW_VALS // SPAN * KEEP
OWN = 8
HIGHEST = lax.Precision.HIGHEST
BOTH = ("dp", "fsdp")
N_DP = 32
N_FSDP = 16


def dct_table_t():
    n = np.arange(SPAN)[:, None]
    k = np.arange(SPAN)[None, :]
    turn = ((2 * n + 1) * k) % (4 * SPAN)
    scale = np.where(k == 0, np.sqrt(1.0 / SPAN), np.sqrt(2.0 / SPAN))
    return scale * np.cos(np.pi * turn / (2 * SPAN))


def spread(table, kept_ref, dtype):
    lane = lax.broadcasted_iota(jnp.int32, (SPAN, 128), 1)
    k = lax.broadcasted_iota(jnp.int32, (SPAN, 128), 0)
    which = jnp.zeros((SPAN, 128), jnp.int32)
    for j in range(KEEP):
        which = jnp.where(lane % KEEP == j, kept_ref[j], which)
    onehot = (which == k).astype(jnp.float32)
    if dtype == jnp.bfloat16:
        picked = jnp.dot(table, onehot.astype(dtype), preferred_element_type=jnp.float32)
    else:
        picked = jnp.dot(table, onehot, precision=HIGHEST, preferred_element_type=jnp.float32)
    tall = jnp.concatenate([picked] * GROUP, axis=0)
    row = lax.broadcasted_iota(jnp.int32, (WIDE, 128), 0)
    col = lax.broadcasted_iota(jnp.int32, (WIDE, 128), 1)
    return jnp.where(row // SPAN == col // KEEP, tall, 0.0).astype(dtype)


def prep_kernel(first, place_ref, kept_ref, hi_ref, lo_ref, grad_ref, main_ref, coef_ref):
    y, z, near, far = place_ref[0], place_ref[1], place_ref[2], place_ref[3]
    shape = (2 * 4 * OWN, 2 * 64)
    r = lax.broadcasted_iota(jnp.int32, shape, 0)
    col = lax.broadcasted_iota(jnp.int32, shape, 1)

    def partner(slot):
        return jnp.where(slot == 0, 0, jnp.where(slot == 1, far, jnp.where(slot == 2, near, 2)))

    to_y = y ^ partner(first + r // (4 * OWN))
    to_z = z ^ partner((r // OWN) % 4)
    source = ((r // 4) % 2) * 64 + to_z * 16 + to_y * 4 + r % 4
    order = (source == col).astype(jnp.float32).astype(jnp.bfloat16)
    wide_hi = spread(hi_ref[...], kept_ref, jnp.bfloat16)
    wide_lo = spread(lo_ref[...], kept_ref, jnp.bfloat16)
    for c in range(CHUNKS):
        values = grad_ref[:, :, c * WIDE:(c + 1) * WIDE].reshape(128, WIDE)
        rows = jnp.dot(order, values, preferred_element_type=jnp.float32)
        main_ref[:, :, :, c * WIDE:(c + 1) * WIDE] = rows.reshape(2, 4, OWN, WIDE)
        exact = rows.astype(jnp.bfloat16)
        coef = jnp.dot(exact, wide_hi, preferred_element_type=jnp.float32)
        coef = coef + jnp.dot(exact, wide_lo, preferred_element_type=jnp.float32)
        coef_ref[:, :, :, c * 128:(c + 1) * 128] = coef.reshape(2, 4, OWN, 128)


def prep(first, place, kept, hi, lo, grad):
    smem = pl.BlockSpec(memory_space=pltpu.SMEM)
    vmem = pl.BlockSpec(memory_space=pltpu.VMEM)
    return pl.pallas_call(
        functools.partial(prep_kernel, first),
        out_shape=(
            jax.ShapeDtypeStruct((2, 4, OWN, ROW_VALS), jnp.float32),
            jax.ShapeDtypeStruct((2, 4, OWN, COEFFS), jnp.float32),
        ),
        in_specs=[smem, smem, vmem, vmem, vmem],
        out_specs=(vmem, vmem),
        compiler_params=pltpu.CompilerParams(vmem_limit_bytes=32 * 2**20),
        cost_estimate=pl.CostEstimate(flops=400_000_000, bytes_accessed=3_000_000, transcendentals=0),
        name="prep",
    )(place, kept, hi, lo, grad)


def tall(x):
    return jnp.concatenate([x[:, c * 128:(c + 1) * 128] for c in range(x.shape[1] // 128)], axis=0)


def state_kernel(kept_ref, table_ref, momentum_ref, coef_ref, reject_ref, expand_ref):
    wide = spread(table_ref[...], kept_ref, jnp.float32)
    pair = wide[:128, :]
    row = lax.broadcasted_iota(jnp.int32, (128, 128), 0)
    col = lax.broadcasted_iota(jnp.int32, (128, 128), 1)
    onto = lax.dot_general(pair, pair, (((1,), (1,)), ((), ())), precision=HIGHEST, preferred_element_type=jnp.float32)
    reject_ref[...] = jnp.where(row == col, 1.0, 0.0) - onto
    expand_ref[...] = wide
    state = 0.9 * jnp.concatenate([momentum_ref[0, 0], momentum_ref[0, 1]], axis=0)
    deep = jnp.concatenate([state[:, c * WIDE:(c + 1) * WIDE] for c in range(CHUNKS)], axis=0)
    coef = jnp.dot(deep, wide, precision=HIGHEST, preferred_element_type=jnp.float32)
    for c in range(CHUNKS):
        coef_ref[:, c * 128:(c + 1) * 128] = coef[c * OWN:(c + 1) * OWN]


def state_of(kept, table, momentum):
    smem = pl.BlockSpec(memory_space=pltpu.SMEM)
    vmem = pl.BlockSpec(memory_space=pltpu.VMEM)
    return pl.pallas_call(
        state_kernel,
        out_shape=(
            jax.ShapeDtypeStruct((OWN, COEFFS), jnp.float32),
            jax.ShapeDtypeStruct((128, 128), jnp.float32),
            jax.ShapeDtypeStruct((WIDE, 128), jnp.float32),
        ),
        in_specs=[smem, vmem, vmem],
        out_specs=(vmem, vmem, vmem),
        compiler_params=pltpu.CompilerParams(vmem_limit_bytes=32 * 2**20),
        cost_estimate=pl.CostEstimate(flops=100_000_000, bytes_accessed=1_000_000, transcendentals=0),
        name="state",
    )(kept, table, momentum)


def momentum_kernel(own_ref, got_ref, momentum_ref, reject_ref, out_ref):
    state = jnp.concatenate([momentum_ref[0, 0], momentum_ref[0, 1]], axis=0)
    moment = 0.9 * state + (own_ref[...] + got_ref[...])
    new = jnp.dot(tall(moment), reject_ref[...], precision=HIGHEST, preferred_element_type=jnp.float32)
    for c in range(ROW_VALS // 128):
        part = new[c * OWN:(c + 1) * OWN]
        out_ref[0, 0, :, c * 128:(c + 1) * 128] = part[:4]
        out_ref[0, 1, :, c * 128:(c + 1) * 128] = part[4:]


def new_momentum_of(own, got, momentum, reject):
    vmem = pl.BlockSpec(memory_space=pltpu.VMEM)
    return pl.pallas_call(
        momentum_kernel,
        out_shape=jax.ShapeDtypeStruct(momentum.shape, jnp.float32),
        in_specs=[vmem] * 4,
        out_specs=vmem,
        compiler_params=pltpu.CompilerParams(vmem_limit_bytes=32 * 2**20),
        cost_estimate=pl.CostEstimate(flops=60_000_000, bytes_accessed=700_000, transcendentals=0),
        name="momentum",
    )(own, got, momentum, reject)


def params_kernel(own_ref, got_ref, params_ref, expand_ref, out_ref):
    shared = (own_ref[...] + got_ref[...]) * (1.0 / N_DP)
    deep = tall(shared)
    update = lax.dot_general(
        deep, expand_ref[...], (((1,), (1,)), ((), ())), precision=HIGHEST, preferred_element_type=jnp.float32
    )
    for c in range(CHUNKS):
        lanes = slice(c * WIDE, (c + 1) * WIDE)
        part = update[c * OWN:(c + 1) * OWN]
        out_ref[0, :, lanes] = params_ref[0, :, lanes] - part[:4]
        out_ref[1, :, lanes] = params_ref[1, :, lanes] - part[4:]


def new_params_of(own, got, params, expand):
    vmem = pl.BlockSpec(memory_space=pltpu.VMEM)
    return pl.pallas_call(
        params_kernel,
        out_shape=jax.ShapeDtypeStruct(params.shape, jnp.float32),
        in_specs=[vmem] * 4,
        out_specs=vmem,
        compiler_params=pltpu.CompilerParams(vmem_limit_bytes=32 * 2**20),
        cost_estimate=pl.CostEstimate(flops=60_000_000, bytes_accessed=700_000, transcendentals=0),
        name="params",
    )(own, got, params, expand)


def sum_pairs(step, axis):
    pairs = []
    for d in range(N_DP):
        flip = (1, 3)[(d % 2) ^ step]
        for f in range(N_FSDP):
            to = f ^ (flip if axis == "y" else 4 * flip)
            pairs.append((d * N_FSDP + f, d * N_FSDP + to))
    return pairs


def halve(x, first, step, axis):
    return lax.ppermute(x, BOTH, sum_pairs(step, axis))


def dp_swap(x, flip):
    return lax.ppermute(x, "dp", [(d, d ^ flip) for d in range(N_DP)])


def scatter_z(x):
    got = lax.ppermute(x[2:], BOTH, sum_pairs(0, "z"))
    last = lax.ppermute(x[1] + got[1], BOTH, sum_pairs(1, "z"))
    return x[0] + got[0], last


def scatter_y(sent, kept):
    got = lax.ppermute(sent, BOTH, sum_pairs(0, "y"))
    last = lax.ppermute(kept[1] + got[1], BOTH, sum_pairs(1, "y"))
    return kept[0] + got[0] + last


def shards(grad_partials, momentum, params, kept):
    place = lax.axis_index("fsdp")
    core = lax.axis_index("dp") % 2
    near = 1 + 2 * core
    place = jnp.stack([place % 4, place // 4, near, 4 - near]).astype(jnp.int32)
    exact = dct_table_t()
    table = jnp.asarray(exact.astype(np.float32))
    hi = np.asarray(exact, jnp.bfloat16)
    lo = np.asarray(exact - hi.astype(np.float64), jnp.bfloat16)
    grad = grad_partials[0, 0]

    main_out, coef_out = prep(2, place, kept, hi, lo, grad)
    main_own, coef_own = prep(0, place, kept, hi, lo, grad)
    state_coef, reject, expand = state_of(kept, table, momentum)

    coef = scatter_y(coef_out, coef_own)
    own, got = scatter_z(coef)
    coef = own + got + state_coef
    for flip in (1, 2, 6, 8):
        coef = coef + dp_swap(coef, flip)
    other = dp_swap(coef, 16)
    new_params = new_params_of(coef, other, params, expand)

    main = scatter_y(main_out, main_own)
    own, got = scatter_z(main)
    new_momentum = new_momentum_of(own, got, momentum, reject)
    return (new_params, new_momentum)


def solution(mesh):
    placed = (
        P("dp", "fsdp", None, None, None),
        P("dp", None, "fsdp", None),
        P(None, "fsdp", None),
        P(),
    )
    return jax.shard_map(
        shards,
        mesh=mesh,
        in_specs=placed,
        out_specs=(P(None, "fsdp", None), P("dp", None, "fsdp", None)),
        check_vma=False,
    )
```

```python
import math

import jax
import jax.numpy as jnp
import numpy as np
from jax import lax
from jax.experimental import pallas as pl
from jax.experimental.pallas import tpu as pltpu
from jax.sharding import PartitionSpec as P

SPAN = 64
KEEP = 8
ROW_VALS = 5120
LAYERS = 2
GROUP = 128 // KEEP
WIDE = GROUP * SPAN
CHUNKS = ROW_VALS // WIDE
COEFFS = ROW_VALS // SPAN * KEEP
OWN = 8
HIGHEST = lax.Precision.HIGHEST
BOTH = ("dp", "fsdp")
N_DP = 32
N_FSDP = 16


def picked_t(kept_ref):
    lane = lax.broadcasted_iota(jnp.int32, (SPAN, 128), 1) % KEEP
    n = lax.broadcasted_iota(jnp.int32, (SPAN, 128), 0)
    k = jnp.zeros((SPAN, 128), jnp.int32)
    for j in range(KEEP):
        k = jnp.where(lane == j, kept_ref[j], k)
    turn = ((2 * n + 1) * k) & (4 * SPAN - 1)
    turn = jnp.minimum(turn, 4 * SPAN - turn)
    flip = turn > SPAN
    angle = jnp.where(flip, 2 * SPAN - turn, turn).astype(jnp.float32) * np.float32(np.pi / (2 * SPAN))
    square = angle * angle
    value = jnp.full((SPAN, 128), (-1.0) ** 8 / math.factorial(16), jnp.float32)
    for term in range(7, -1, -1):
        value = value * square + (-1.0) ** term / math.factorial(2 * term)
    value = jnp.where(flip, -value, value)
    return value * jnp.where(k == 0, np.float32(np.sqrt(1.0 / SPAN)), np.float32(np.sqrt(2.0 / SPAN)))


def spread(picked):
    tall = jnp.concatenate([picked] * GROUP, axis=0)
    row = lax.broadcasted_iota(jnp.int32, (WIDE, 128), 0)
    col = lax.broadcasted_iota(jnp.int32, (WIDE, 128), 1)
    return jnp.where(row // SPAN == col // KEEP, tall, 0.0)


def slot_order():
    y, z = lax.axis_index("fsdp") % 4, lax.axis_index("fsdp") // 4
    near = 1 + 2 * (lax.axis_index("dp") % 2)
    far = 4 - near
    r = lax.broadcasted_iota(jnp.int32, (128, 128), 0)
    col = lax.broadcasted_iota(jnp.int32, (128, 128), 1)

    def partner(slot):
        return jnp.where(slot == 0, 0, jnp.where(slot == 1, far, jnp.where(slot == 2, near, 2)))

    to_y = y ^ partner(r // (4 * OWN))
    to_z = z ^ partner((r // OWN) % 4)
    source = ((r // 4) % 2) * 64 + to_z * 16 + to_y * 4 + r % 4
    return (source == col).astype(jnp.float32).astype(jnp.bfloat16)


def coef_kernel(indices_ref, grad_ref, kept_out_ref, sent_ref, kept_ref, held, sems):
    indices = pltpu.make_async_copy(indices_ref, kept_ref, sems.at[CHUNKS])
    indices.start()

    def chunk(c):
        lanes = pl.ds(c * WIDE, WIDE)
        return pltpu.make_async_copy(grad_ref.at[:, :, lanes], held.at[:, :, lanes], sems.at[c])

    for c in range(CHUNKS):
        chunk(c).start()
    order = slot_order()
    indices.wait()
    picked = picked_t(kept_ref)
    high = picked.astype(jnp.bfloat16).astype(jnp.float32)
    wide_hi = spread(high).astype(jnp.bfloat16)
    wide_lo = spread(picked - high).astype(jnp.bfloat16)
    for c in range(CHUNKS):
        chunk(c).wait()
        values = held[:, :, c * WIDE:(c + 1) * WIDE].reshape(128, WIDE)
        exact = jnp.dot(order, values, preferred_element_type=jnp.float32).astype(jnp.bfloat16)
        coef = jnp.dot(exact, wide_hi, preferred_element_type=jnp.float32)
        coef = coef + jnp.dot(exact, wide_lo, preferred_element_type=jnp.float32)
        kept_out_ref[:, :, :, c * 128:(c + 1) * 128] = coef[:64].reshape(2, 4, OWN, 128)
        sent_ref[:, :, :, c * 128:(c + 1) * 128] = coef[64:].reshape(2, 4, OWN, 128)


def coef_of(kept, grad):
    hbm = pl.BlockSpec(memory_space=pltpu.HBM)
    vmem = pl.BlockSpec(memory_space=pltpu.VMEM)
    half = jax.ShapeDtypeStruct((2, 4, OWN, COEFFS), jnp.float32)
    return pl.pallas_call(
        coef_kernel,
        out_shape=(half, half),
        in_specs=[hbm, hbm],
        out_specs=(vmem, vmem),
        scratch_shapes=[
            pltpu.SMEM(kept.shape, kept.dtype),
            pltpu.VMEM(grad.shape, grad.dtype),
            pltpu.SemaphoreType.DMA((CHUNKS + 1,)),
        ],
        compiler_params=pltpu.CompilerParams(vmem_limit_bytes=32 * 2**20),
        cost_estimate=pl.CostEstimate(flops=500_000_000, bytes_accessed=2_000_000, transcendentals=0),
        name="coef",
    )(kept, grad)


def main_kernel(grad_ref, kept_ref, sent_ref):
    order = slot_order()
    for c in range(CHUNKS):
        lanes = slice(c * WIDE, (c + 1) * WIDE)
        values = grad_ref[:, :, lanes].reshape(128, WIDE)
        rows = jnp.dot(order, values, preferred_element_type=jnp.float32)
        kept_ref[:, :, :, lanes] = rows[:64].reshape(2, 4, OWN, WIDE)
        sent_ref[:, :, :, lanes] = rows[64:].reshape(2, 4, OWN, WIDE)


def main_of(grad):
    vmem = pl.BlockSpec(memory_space=pltpu.VMEM)
    half = jax.ShapeDtypeStruct((2, 4, OWN, ROW_VALS), jnp.float32)
    return pl.pallas_call(
        main_kernel,
        out_shape=(half, half),
        in_specs=[vmem],
        out_specs=(vmem, vmem),
        compiler_params=pltpu.CompilerParams(vmem_limit_bytes=32 * 2**20),
        cost_estimate=pl.CostEstimate(flops=200_000_000, bytes_accessed=4_000_000, transcendentals=0),
        name="main",
    )(grad)


def tall(x):
    return jnp.concatenate([x[:, c * 128:(c + 1) * 128] for c in range(x.shape[1] // 128)], axis=0)


def state_kernel(kept_ref, momentum_ref, coef_ref, reject_ref, expand_ref):
    wide = spread(picked_t(kept_ref))
    pair = wide[:128, :]
    row = lax.broadcasted_iota(jnp.int32, (128, 128), 0)
    col = lax.broadcasted_iota(jnp.int32, (128, 128), 1)
    onto = lax.dot_general(pair, pair, (((1,), (1,)), ((), ())), precision=HIGHEST, preferred_element_type=jnp.float32)
    reject_ref[...] = jnp.where(row == col, 1.0, 0.0) - onto
    expand_ref[...] = wide
    state = 0.9 * jnp.concatenate([momentum_ref[0, 0], momentum_ref[0, 1]], axis=0)
    deep = jnp.concatenate([state[:, c * WIDE:(c + 1) * WIDE] for c in range(CHUNKS)], axis=0)
    coef = jnp.dot(deep, wide, precision=HIGHEST, preferred_element_type=jnp.float32)
    for c in range(CHUNKS):
        coef_ref[:, c * 128:(c + 1) * 128] = coef[c * OWN:(c + 1) * OWN]


def state_of(kept, momentum):
    smem = pl.BlockSpec(memory_space=pltpu.SMEM)
    vmem = pl.BlockSpec(memory_space=pltpu.VMEM)
    return pl.pallas_call(
        state_kernel,
        out_shape=(
            jax.ShapeDtypeStruct((OWN, COEFFS), jnp.float32),
            jax.ShapeDtypeStruct((128, 128), jnp.float32),
            jax.ShapeDtypeStruct((WIDE, 128), jnp.float32),
        ),
        in_specs=[smem, vmem],
        out_specs=(vmem, vmem, vmem),
        compiler_params=pltpu.CompilerParams(vmem_limit_bytes=32 * 2**20),
        cost_estimate=pl.CostEstimate(flops=100_000_000, bytes_accessed=1_000_000, transcendentals=0),
        name="state",
    )(kept, momentum)


def momentum_kernel(own_ref, got_ref, momentum_ref, reject_ref, out_ref):
    state = jnp.concatenate([momentum_ref[0, 0], momentum_ref[0, 1]], axis=0)
    moment = 0.9 * state + (own_ref[...] + got_ref[...])
    new = jnp.dot(tall(moment), reject_ref[...], precision=HIGHEST, preferred_element_type=jnp.float32)
    for c in range(ROW_VALS // 128):
        part = new[c * OWN:(c + 1) * OWN]
        out_ref[0, 0, :, c * 128:(c + 1) * 128] = part[:4]
        out_ref[0, 1, :, c * 128:(c + 1) * 128] = part[4:]


def new_momentum_of(own, got, momentum, reject):
    vmem = pl.BlockSpec(memory_space=pltpu.VMEM)
    return pl.pallas_call(
        momentum_kernel,
        out_shape=jax.ShapeDtypeStruct(momentum.shape, jnp.float32),
        in_specs=[vmem] * 4,
        out_specs=vmem,
        compiler_params=pltpu.CompilerParams(vmem_limit_bytes=32 * 2**20),
        cost_estimate=pl.CostEstimate(flops=60_000_000, bytes_accessed=700_000, transcendentals=0),
        name="momentum",
    )(own, got, momentum, reject)


def params_kernel(own_ref, got_ref, params_ref, expand_ref, out_ref):
    shared = (own_ref[...] + got_ref[...]) * (1.0 / N_DP)
    deep = tall(shared)
    update = lax.dot_general(
        deep, expand_ref[...], (((1,), (1,)), ((), ())), precision=HIGHEST, preferred_element_type=jnp.float32
    )
    for c in range(CHUNKS):
        lanes = slice(c * WIDE, (c + 1) * WIDE)
        part = update[c * OWN:(c + 1) * OWN]
        out_ref[0, :, lanes] = params_ref[0, :, lanes] - part[:4]
        out_ref[1, :, lanes] = params_ref[1, :, lanes] - part[4:]


def new_params_of(own, got, params, expand):
    vmem = pl.BlockSpec(memory_space=pltpu.VMEM)
    return pl.pallas_call(
        params_kernel,
        out_shape=jax.ShapeDtypeStruct(params.shape, jnp.float32),
        in_specs=[vmem] * 4,
        out_specs=vmem,
        compiler_params=pltpu.CompilerParams(vmem_limit_bytes=32 * 2**20),
        cost_estimate=pl.CostEstimate(flops=60_000_000, bytes_accessed=700_000, transcendentals=0),
        name="params",
    )(own, got, params, expand)


def sum_pairs(step, axis):
    pairs = []
    for d in range(N_DP):
        flip = (1, 3)[(d % 2) ^ step]
        for f in range(N_FSDP):
            to = f ^ (flip if axis == "y" else 4 * flip)
            pairs.append((d * N_FSDP + f, d * N_FSDP + to))
    return pairs


def halve(x, step, axis):
    return lax.ppermute(x, BOTH, sum_pairs(step, axis))


def dp_swap(x, flip):
    return lax.ppermute(x, "dp", [(d, d ^ flip) for d in range(N_DP)])


def after(x, earlier):
    return lax.optimization_barrier((x, earlier))


def shards(grad_partials, momentum, params, kept):
    grad = grad_partials[0, 0]
    coef, coef_sent = coef_of(kept, grad)
    main, main_sent = main_of(grad)
    state_coef, reject, expand = state_of(kept, momentum)

    coef_got = halve(coef_sent, 0, "y")
    main_sent, coef_got = after(main_sent, coef_got)
    main_got = halve(main_sent, 0, "y")
    coef_last = halve(coef[1] + coef_got[1], 1, "y")
    coef = coef[0] + coef_got[0] + coef_last
    coef_got = halve(coef[2:], 0, "z")
    main_got, coef_got = after(main_got, coef_got)

    main_last = halve(main[1] + main_got[1], 1, "y")
    coef_last = halve(coef[1] + coef_got[1], 1, "z")
    coef = coef[0] + coef_got[0] + coef_last + state_coef
    coef = coef + dp_swap(coef, 1)
    main_last, coef = after(main_last, coef)

    main = main[0] + main_got[0] + main_last
    main_got = halve(main[2:], 0, "z")
    for flip in (2, 6, 8):
        coef = coef + dp_swap(coef, flip)
    main_got, coef = after(main_got, coef)

    main_last = halve(main[1] + main_got[1], 1, "z")
    other = dp_swap(coef, 16)
    new_params = new_params_of(coef, other, params, expand)
    main_last, new_params = after(main_last, new_params)
    new_momentum = new_momentum_of(main[0] + main_got[0], main_last, momentum, reject)
    return (new_params, new_momentum)


def solution(mesh):
    placed = (
        P("dp", "fsdp", None, None, None),
        P("dp", None, "fsdp", None),
        P(None, "fsdp", None),
        P(),
    )
    return jax.shard_map(
        shards,
        mesh=mesh,
        in_specs=placed,
        out_specs=(P(None, "fsdp", None), P("dp", None, "fsdp", None)),
        check_vma=False,
    )
```

```python
import math

import jax
import jax.numpy as jnp
import numpy as np
from jax import lax
from jax.experimental import pallas as pl
from jax.experimental.pallas import tpu as pltpu
from jax.sharding import PartitionSpec as P

SPAN = 64
KEEP = 8
ROW_VALS = 5120
LAYERS = 2
GROUP = 128 // KEEP
WIDE = GROUP * SPAN
CHUNKS = ROW_VALS // WIDE
COEFFS = ROW_VALS // SPAN * KEEP
OWN = 8
HIGHEST = lax.Precision.HIGHEST
BOTH = ("dp", "fsdp")
N_DP = 32
N_FSDP = 16


def picked_t(kept_ref):
    lane = lax.broadcasted_iota(jnp.int32, (SPAN, 128), 1) % KEEP
    n = lax.broadcasted_iota(jnp.int32, (SPAN, 128), 0)
    k = jnp.zeros((SPAN, 128), jnp.int32)
    for j in range(KEEP):
        k = jnp.where(lane == j, kept_ref[j], k)
    turn = ((2 * n + 1) * k) & (4 * SPAN - 1)
    turn = jnp.minimum(turn, 4 * SPAN - turn)
    flip = turn > SPAN
    angle = jnp.where(flip, 2 * SPAN - turn, turn).astype(jnp.float32) * np.float32(np.pi / (2 * SPAN))
    square = angle * angle
    value = jnp.full((SPAN, 128), (-1.0) ** 8 / math.factorial(16), jnp.float32)
    for term in range(7, -1, -1):
        value = value * square + (-1.0) ** term / math.factorial(2 * term)
    value = jnp.where(flip, -value, value)
    return value * jnp.where(k == 0, np.float32(np.sqrt(1.0 / SPAN)), np.float32(np.sqrt(2.0 / SPAN)))


def spread(picked):
    tall = jnp.concatenate([picked] * GROUP, axis=0)
    row = lax.broadcasted_iota(jnp.int32, (WIDE, 128), 0)
    col = lax.broadcasted_iota(jnp.int32, (WIDE, 128), 1)
    return jnp.where(row // SPAN == col // KEEP, tall, 0.0)


def row_order():
    r = lax.broadcasted_iota(jnp.int32, (128, 128), 0)
    col = lax.broadcasted_iota(jnp.int32, (128, 128), 1)
    source = ((r // 4) % 2) * 64 + ((r // OWN) % 4) * 16 + (r // (4 * OWN)) * 4 + r % 4
    return (source == col).astype(jnp.float32).astype(jnp.bfloat16)


def slot_order():
    y, z = lax.axis_index("fsdp") % 4, lax.axis_index("fsdp") // 4
    near = 1 + 2 * (lax.axis_index("dp") % 2)
    far = 4 - near
    r = lax.broadcasted_iota(jnp.int32, (128, 128), 0)
    col = lax.broadcasted_iota(jnp.int32, (128, 128), 1)

    def partner(slot):
        return jnp.where(slot == 0, 0, jnp.where(slot == 1, far, jnp.where(slot == 2, near, 2)))

    to_y = y ^ partner(r // (4 * OWN))
    to_z = z ^ partner((r // OWN) % 4)
    source = ((r // 4) % 2) * 64 + to_z * 16 + to_y * 4 + r % 4
    return (source == col).astype(jnp.float32).astype(jnp.bfloat16)


def coef_kernel(indices_ref, grad_ref, coef_ref, kept_ref, held, sems):
    indices = pltpu.make_async_copy(indices_ref, kept_ref, sems.at[CHUNKS])
    indices.start()

    def chunk(c):
        lanes = pl.ds(c * WIDE, WIDE)
        return pltpu.make_async_copy(grad_ref.at[:, :, lanes], held.at[:, :, lanes], sems.at[c])

    for c in range(CHUNKS):
        chunk(c).start()
    order = row_order()
    indices.wait()
    picked = picked_t(kept_ref)
    high = picked.astype(jnp.bfloat16).astype(jnp.float32)
    wide_hi = spread(high).astype(jnp.bfloat16)
    wide_lo = spread(picked - high).astype(jnp.bfloat16)
    for c in range(CHUNKS):
        chunk(c).wait()
        values = held[:, :, c * WIDE:(c + 1) * WIDE].reshape(128, WIDE)
        exact = jnp.dot(order, values, preferred_element_type=jnp.float32).astype(jnp.bfloat16)
        coef = jnp.dot(exact, wide_hi, preferred_element_type=jnp.float32)
        coef = coef + jnp.dot(exact, wide_lo, preferred_element_type=jnp.float32)
        coef_ref[:, :, :, c * 128:(c + 1) * 128] = coef.reshape(4, 4, OWN, 128)


def coef_of(kept, grad):
    hbm = pl.BlockSpec(memory_space=pltpu.HBM)
    vmem = pl.BlockSpec(memory_space=pltpu.VMEM)
    return pl.pallas_call(
        coef_kernel,
        out_shape=jax.ShapeDtypeStruct((4, 4, OWN, COEFFS), jnp.float32),
        in_specs=[hbm, hbm],
        out_specs=vmem,
        scratch_shapes=[
            pltpu.SMEM(kept.shape, kept.dtype),
            pltpu.VMEM(grad.shape, grad.dtype),
            pltpu.SemaphoreType.DMA((CHUNKS + 1,)),
        ],
        compiler_params=pltpu.CompilerParams(vmem_limit_bytes=32 * 2**20),
        cost_estimate=pl.CostEstimate(flops=500_000_000, bytes_accessed=2_000_000, transcendentals=0),
        name="coef",
    )(kept, grad)


def main_kernel(grad_ref, kept_ref, sent_ref):
    order = slot_order()
    for c in range(CHUNKS):
        lanes = slice(c * WIDE, (c + 1) * WIDE)
        values = grad_ref[:, :, lanes].reshape(128, WIDE)
        rows = jnp.dot(order, values, preferred_element_type=jnp.float32)
        kept_ref[:, :, :, lanes] = rows[:64].reshape(2, 4, OWN, WIDE)
        sent_ref[:, :, :, lanes] = rows[64:].reshape(2, 4, OWN, WIDE)


def main_of(grad):
    vmem = pl.BlockSpec(memory_space=pltpu.VMEM)
    half = jax.ShapeDtypeStruct((2, 4, OWN, ROW_VALS), jnp.float32)
    return pl.pallas_call(
        main_kernel,
        out_shape=(half, half),
        in_specs=[vmem],
        out_specs=(vmem, vmem),
        compiler_params=pltpu.CompilerParams(vmem_limit_bytes=32 * 2**20),
        cost_estimate=pl.CostEstimate(flops=200_000_000, bytes_accessed=4_000_000, transcendentals=0),
        name="main",
    )(grad)


def tall(x):
    return jnp.concatenate([x[:, c * 128:(c + 1) * 128] for c in range(x.shape[1] // 128)], axis=0)


def state_kernel(kept_ref, momentum_ref, coef_ref, reject_ref, expand_ref):
    wide = spread(picked_t(kept_ref))
    pair = wide[:128, :]
    row = lax.broadcasted_iota(jnp.int32, (128, 128), 0)
    col = lax.broadcasted_iota(jnp.int32, (128, 128), 1)
    onto = lax.dot_general(pair, pair, (((1,), (1,)), ((), ())), precision=HIGHEST, preferred_element_type=jnp.float32)
    reject_ref[...] = jnp.where(row == col, 1.0, 0.0) - onto
    expand_ref[...] = wide
    state = 0.9 * jnp.concatenate([momentum_ref[0, 0], momentum_ref[0, 1]], axis=0)
    deep = jnp.concatenate([state[:, c * WIDE:(c + 1) * WIDE] for c in range(CHUNKS)], axis=0)
    coef = jnp.dot(deep, wide, precision=HIGHEST, preferred_element_type=jnp.float32)
    for c in range(CHUNKS):
        coef_ref[:, c * 128:(c + 1) * 128] = coef[c * OWN:(c + 1) * OWN]


def state_of(kept, momentum):
    smem = pl.BlockSpec(memory_space=pltpu.SMEM)
    vmem = pl.BlockSpec(memory_space=pltpu.VMEM)
    return pl.pallas_call(
        state_kernel,
        out_shape=(
            jax.ShapeDtypeStruct((OWN, COEFFS), jnp.float32),
            jax.ShapeDtypeStruct((128, 128), jnp.float32),
            jax.ShapeDtypeStruct((WIDE, 128), jnp.float32),
        ),
        in_specs=[smem, vmem],
        out_specs=(vmem, vmem, vmem),
        compiler_params=pltpu.CompilerParams(vmem_limit_bytes=32 * 2**20),
        cost_estimate=pl.CostEstimate(flops=100_000_000, bytes_accessed=1_000_000, transcendentals=0),
        name="state",
    )(kept, momentum)


def momentum_kernel(own_ref, got_ref, momentum_ref, reject_ref, out_ref):
    state = jnp.concatenate([momentum_ref[0, 0], momentum_ref[0, 1]], axis=0)
    moment = 0.9 * state + (own_ref[...] + got_ref[...])
    new = jnp.dot(tall(moment), reject_ref[...], precision=HIGHEST, preferred_element_type=jnp.float32)
    for c in range(ROW_VALS // 128):
        part = new[c * OWN:(c + 1) * OWN]
        out_ref[0, 0, :, c * 128:(c + 1) * 128] = part[:4]
        out_ref[0, 1, :, c * 128:(c + 1) * 128] = part[4:]


def new_momentum_of(own, got, momentum, reject):
    vmem = pl.BlockSpec(memory_space=pltpu.VMEM)
    return pl.pallas_call(
        momentum_kernel,
        out_shape=jax.ShapeDtypeStruct(momentum.shape, jnp.float32),
        in_specs=[vmem] * 4,
        out_specs=vmem,
        compiler_params=pltpu.CompilerParams(vmem_limit_bytes=32 * 2**20),
        cost_estimate=pl.CostEstimate(flops=60_000_000, bytes_accessed=700_000, transcendentals=0),
        name="momentum",
    )(own, got, momentum, reject)


def params_kernel(total_ref, params_ref, expand_ref, out_ref):
    shared = total_ref[...] * (1.0 / N_DP)
    deep = tall(shared)
    update = lax.dot_general(
        deep, expand_ref[...], (((1,), (1,)), ((), ())), precision=HIGHEST, preferred_element_type=jnp.float32
    )
    for c in range(CHUNKS):
        lanes = slice(c * WIDE, (c + 1) * WIDE)
        part = update[c * OWN:(c + 1) * OWN]
        out_ref[0, :, lanes] = params_ref[0, :, lanes] - part[:4]
        out_ref[1, :, lanes] = params_ref[1, :, lanes] - part[4:]


def new_params_of(total, params, expand):
    vmem = pl.BlockSpec(memory_space=pltpu.VMEM)
    return pl.pallas_call(
        params_kernel,
        out_shape=jax.ShapeDtypeStruct(params.shape, jnp.float32),
        in_specs=[vmem] * 3,
        out_specs=vmem,
        compiler_params=pltpu.CompilerParams(vmem_limit_bytes=32 * 2**20),
        cost_estimate=pl.CostEstimate(flops=60_000_000, bytes_accessed=700_000, transcendentals=0),
        name="params",
    )(total, params, expand)


def sum_pairs(step, axis):
    pairs = []
    for d in range(N_DP):
        flip = (1, 3)[(d % 2) ^ step]
        for f in range(N_FSDP):
            to = f ^ (flip if axis == "y" else 4 * flip)
            pairs.append((d * N_FSDP + f, d * N_FSDP + to))
    return pairs


def halve(x, step, axis):
    return lax.ppermute(x, BOTH, sum_pairs(step, axis))


def sum_over(x, axis, groups):
    return jnp.sum(lax.all_to_all(x, axis, 0, 0, tiled=True, axis_index_groups=groups), axis=0)


def share(x, groups):
    return sum_over(jnp.broadcast_to(x, (len(groups[0]), *x.shape)), "dp", groups)


Y_GROUPS = [[z * 4 + y for y in range(4)] for z in range(4)]
Z_GROUPS = [[z * 4 + y for z in range(4)] for y in range(4)]
PLANE_GROUPS = [[z * 8 + i for i in range(8)] for z in range(4)]
COLUMN_GROUPS = [[z * 8 + i for z in range(4)] for i in range(8)]


def after(x, earlier):
    return lax.optimization_barrier((x, earlier))


def shards(grad_partials, momentum, params, kept):
    grad = grad_partials[0, 0]
    main, main_sent = main_of(grad)
    main_got = halve(main_sent, 0, "y")
    coef = coef_of(kept, grad)
    state_coef, reject, expand = state_of(kept, momentum)
    coef = sum_over(coef, "fsdp", Y_GROUPS)
    main_got, coef = after(main_got, coef)

    main_last = halve(main[1] + main_got[1], 1, "y")
    coef = sum_over(coef, "fsdp", Z_GROUPS) + state_coef
    main_last, coef = after(main_last, coef)

    main = main[0] + main_got[0] + main_last
    main_got = halve(main[2:], 0, "z")
    coef = share(coef, PLANE_GROUPS)
    main_got, coef = after(main_got, coef)

    main_last = halve(main[1] + main_got[1], 1, "z")
    coef = share(coef, COLUMN_GROUPS)
    new_params = new_params_of(coef, params, expand)
    main_last, new_params = after(main_last, new_params)
    new_momentum = new_momentum_of(main[0] + main_got[0], main_last, momentum, reject)
    return (new_params, new_momentum)


def solution(mesh):
    placed = (
        P("dp", "fsdp", None, None, None),
        P("dp", None, "fsdp", None),
        P(None, "fsdp", None),
        P(),
    )
    return jax.shard_map(
        shards,
        mesh=mesh,
        in_specs=placed,
        out_specs=(P(None, "fsdp", None), P("dp", None, "fsdp", None)),
        check_vma=False,
    )
```

```python
import math

import jax
import jax.numpy as jnp
import numpy as np
from jax import lax
from jax.experimental import pallas as pl
from jax.experimental.pallas import tpu as pltpu
from jax.sharding import PartitionSpec as P

SPAN = 64
KEEP = 8
ROW_VALS = 5120
LAYERS = 2
GROUP = 128 // KEEP
WIDE = GROUP * SPAN
CHUNKS = ROW_VALS // WIDE
COEFFS = ROW_VALS // SPAN * KEEP
HEAD = 1280
OWN = 8
HIGHEST = lax.Precision.HIGHEST
BOTH = ("dp", "fsdp")
N_DP = 32
N_FSDP = 16


def picked_t(kept_ref):
    lane = lax.broadcasted_iota(jnp.int32, (SPAN, 128), 1) % KEEP
    n = lax.broadcasted_iota(jnp.int32, (SPAN, 128), 0)
    k = jnp.zeros((SPAN, 128), jnp.int32)
    for j in range(KEEP):
        k = jnp.where(lane == j, kept_ref[j], k)
    turn = ((2 * n + 1) * k) & (4 * SPAN - 1)
    turn = jnp.minimum(turn, 4 * SPAN - turn)
    flip = turn > SPAN
    angle = jnp.where(flip, 2 * SPAN - turn, turn).astype(jnp.float32) * np.float32(np.pi / (2 * SPAN))
    square = angle * angle
    value = jnp.full((SPAN, 128), (-1.0) ** 8 / math.factorial(16), jnp.float32)
    for term in range(7, -1, -1):
        value = value * square + (-1.0) ** term / math.factorial(2 * term)
    value = jnp.where(flip, -value, value)
    return value * jnp.where(k == 0, np.float32(np.sqrt(1.0 / SPAN)), np.float32(np.sqrt(2.0 / SPAN)))


def spread(picked):
    tall = jnp.concatenate([picked] * GROUP, axis=0)
    row = lax.broadcasted_iota(jnp.int32, (WIDE, 128), 0)
    col = lax.broadcasted_iota(jnp.int32, (WIDE, 128), 1)
    return jnp.where(row // SPAN == col // KEEP, tall, 0.0)


def slot_order():
    y, z = lax.axis_index("fsdp") % 4, lax.axis_index("fsdp") // 4
    near = 1 + 2 * (lax.axis_index("dp") % 2)
    far = 4 - near
    r = lax.broadcasted_iota(jnp.int32, (128, 128), 0)
    col = lax.broadcasted_iota(jnp.int32, (128, 128), 1)

    def partner(slot):
        return jnp.where(slot == 0, 0, jnp.where(slot == 1, far, jnp.where(slot == 2, near, 2)))

    to_y = y ^ partner(r // (4 * OWN))
    to_z = z ^ partner((r // OWN) % 4)
    source = ((r // 4) % 2) * 64 + to_z * 16 + to_y * 4 + r % 4
    return (source == col).astype(jnp.float32).astype(jnp.bfloat16)


def first_kernel(indices_ref, grad_ref, rest_ref, sent_ref, kept_ref, held, sems):
    def chunk(c):
        lanes = pl.ds(c * WIDE, WIDE)
        return pltpu.make_async_copy(grad_ref.at[:, :, lanes], held.at[:, :, lanes], sems.at[c])

    indices = pltpu.make_async_copy(indices_ref, kept_ref, sems.at[CHUNKS])
    indices.start()
    for c in range(CHUNKS):
        chunk(c).start()
    order = slot_order()
    indices.wait()
    picked = picked_t(kept_ref)
    high = picked.astype(jnp.bfloat16).astype(jnp.float32)
    wide = jnp.concatenate([spread(high), spread(picked - high)], axis=1).astype(jnp.bfloat16)

    def put(lanes, rows):
        rest_ref[:, :, :, lanes] = rows[:64].reshape(2, 4, OWN, rows.shape[1])
        sent_ref[:, :, :, lanes] = rows[64:].reshape(2, 4, OWN, rows.shape[1])

    for c in range(CHUNKS):
        chunk(c).wait()
        values = held[:, :, c * WIDE:(c + 1) * WIDE].reshape(128, WIDE)
        rows = jnp.dot(order, values, preferred_element_type=jnp.float32)
        coef = jnp.dot(rows.astype(jnp.bfloat16), wide, preferred_element_type=jnp.float32)
        put(slice(c * 128, (c + 1) * 128), coef[:, :128] + coef[:, 128:])
        head = min(HEAD - c * WIDE, WIDE)
        if head > 0:
            put(slice(COEFFS + c * WIDE, COEFFS + c * WIDE + head), rows[:, :head])


def first_of(kept, grad):
    hbm = pl.BlockSpec(memory_space=pltpu.HBM)
    vmem = pl.BlockSpec(memory_space=pltpu.VMEM)
    half = jax.ShapeDtypeStruct((2, 4, OWN, COEFFS + HEAD), jnp.float32)
    return pl.pallas_call(
        first_kernel,
        out_shape=(half, half),
        in_specs=[hbm, hbm],
        out_specs=(vmem, vmem),
        scratch_shapes=[
            pltpu.SMEM(kept.shape, kept.dtype),
            pltpu.VMEM(grad.shape, grad.dtype),
            pltpu.SemaphoreType.DMA((CHUNKS + 1,)),
        ],
        compiler_params=pltpu.CompilerParams(vmem_limit_bytes=32 * 2**20),
        cost_estimate=pl.CostEstimate(flops=500_000_000, bytes_accessed=3_000_000, transcendentals=0),
        name="first",
    )(kept, grad)


def second_kernel(grad_ref, rest_ref, sent_ref):
    order = slot_order()
    for start in range(HEAD, ROW_VALS, WIDE):
        lanes = slice(start, min(start + WIDE, ROW_VALS))
        width = lanes.stop - lanes.start
        values = grad_ref[:, :, lanes].reshape(128, width)
        rows = jnp.dot(order, values, preferred_element_type=jnp.float32)
        at = slice(start - HEAD, start - HEAD + width)
        rest_ref[:, :, :, at] = rows[:64].reshape(2, 4, OWN, width)
        sent_ref[:, :, :, at] = rows[64:].reshape(2, 4, OWN, width)


def second_of(grad):
    vmem = pl.BlockSpec(memory_space=pltpu.VMEM)
    half = jax.ShapeDtypeStruct((2, 4, OWN, ROW_VALS - HEAD), jnp.float32)
    return pl.pallas_call(
        second_kernel,
        out_shape=(half, half),
        in_specs=[vmem],
        out_specs=(vmem, vmem),
        compiler_params=pltpu.CompilerParams(vmem_limit_bytes=32 * 2**20),
        cost_estimate=pl.CostEstimate(flops=200_000_000, bytes_accessed=4_000_000, transcendentals=0),
        name="second",
    )(grad)


def tall(x):
    return jnp.concatenate([x[:, c * 128:(c + 1) * 128] for c in range(x.shape[1] // 128)], axis=0)


def state_kernel(kept_ref, momentum_ref, coef_ref, reject_ref, expand_ref):
    wide = spread(picked_t(kept_ref))
    pair = wide[:128, :]
    row = lax.broadcasted_iota(jnp.int32, (128, 128), 0)
    col = lax.broadcasted_iota(jnp.int32, (128, 128), 1)
    onto = lax.dot_general(pair, pair, (((1,), (1,)), ((), ())), precision=HIGHEST, preferred_element_type=jnp.float32)
    reject_ref[...] = jnp.where(row == col, 1.0, 0.0) - onto
    expand_ref[...] = wide
    state = 0.9 * jnp.concatenate([momentum_ref[0, 0], momentum_ref[0, 1]], axis=0)
    deep = jnp.concatenate([state[:, c * WIDE:(c + 1) * WIDE] for c in range(CHUNKS)], axis=0)
    coef = jnp.dot(deep, wide, precision=HIGHEST, preferred_element_type=jnp.float32)
    for c in range(CHUNKS):
        coef_ref[:, c * 128:(c + 1) * 128] = coef[c * OWN:(c + 1) * OWN]


def state_of(kept, momentum):
    smem = pl.BlockSpec(memory_space=pltpu.SMEM)
    vmem = pl.BlockSpec(memory_space=pltpu.VMEM)
    return pl.pallas_call(
        state_kernel,
        out_shape=(
            jax.ShapeDtypeStruct((OWN, COEFFS), jnp.float32),
            jax.ShapeDtypeStruct((128, 128), jnp.float32),
            jax.ShapeDtypeStruct((WIDE, 128), jnp.float32),
        ),
        in_specs=[smem, vmem],
        out_specs=(vmem, vmem, vmem),
        compiler_params=pltpu.CompilerParams(vmem_limit_bytes=32 * 2**20),
        cost_estimate=pl.CostEstimate(flops=100_000_000, bytes_accessed=1_000_000, transcendentals=0),
        name="state",
    )(kept, momentum)


def momentum_kernel(own1_ref, got1_ref, own2_ref, got2_ref, momentum_ref, reject_ref, out_ref):
    state = jnp.concatenate([momentum_ref[0, 0], momentum_ref[0, 1]], axis=0)
    head = own1_ref[:, COEFFS:] + got1_ref[:, COEFFS:]
    grad = jnp.concatenate([head, own2_ref[...] + got2_ref[...]], axis=1)
    moment = 0.9 * state + grad
    new = jnp.dot(tall(moment), reject_ref[...], precision=HIGHEST, preferred_element_type=jnp.float32)
    for c in range(ROW_VALS // 128):
        part = new[c * OWN:(c + 1) * OWN]
        out_ref[0, 0, :, c * 128:(c + 1) * 128] = part[:4]
        out_ref[0, 1, :, c * 128:(c + 1) * 128] = part[4:]


def new_momentum_of(first, second, momentum, reject):
    vmem = pl.BlockSpec(memory_space=pltpu.VMEM)
    return pl.pallas_call(
        momentum_kernel,
        out_shape=jax.ShapeDtypeStruct(momentum.shape, jnp.float32),
        in_specs=[vmem] * 6,
        out_specs=vmem,
        compiler_params=pltpu.CompilerParams(vmem_limit_bytes=32 * 2**20),
        cost_estimate=pl.CostEstimate(flops=60_000_000, bytes_accessed=700_000, transcendentals=0),
        name="momentum",
    )(*first, *second, momentum, reject)


def params_kernel(total_ref, params_ref, expand_ref, out_ref):
    shared = total_ref[...] * (1.0 / N_DP)
    deep = tall(shared)
    update = lax.dot_general(
        deep, expand_ref[...], (((1,), (1,)), ((), ())), precision=HIGHEST, preferred_element_type=jnp.float32
    )
    for c in range(CHUNKS):
        lanes = slice(c * WIDE, (c + 1) * WIDE)
        part = update[c * OWN:(c + 1) * OWN]
        out_ref[0, :, lanes] = params_ref[0, :, lanes] - part[:4]
        out_ref[1, :, lanes] = params_ref[1, :, lanes] - part[4:]


def new_params_of(total, params, expand):
    vmem = pl.BlockSpec(memory_space=pltpu.VMEM)
    return pl.pallas_call(
        params_kernel,
        out_shape=jax.ShapeDtypeStruct(params.shape, jnp.float32),
        in_specs=[vmem] * 3,
        out_specs=vmem,
        compiler_params=pltpu.CompilerParams(vmem_limit_bytes=32 * 2**20),
        cost_estimate=pl.CostEstimate(flops=60_000_000, bytes_accessed=700_000, transcendentals=0),
        name="params",
    )(total, params, expand)


def sum_pairs(step, axis):
    pairs = []
    for d in range(N_DP):
        flip = (1, 3)[(d % 2) ^ step]
        for f in range(N_FSDP):
            to = f ^ (flip if axis == "y" else 4 * flip)
            pairs.append((d * N_FSDP + f, d * N_FSDP + to))
    return pairs


def halve(x, step, axis):
    return lax.ppermute(x, BOTH, sum_pairs(step, axis))


def sum_over(x, axis, groups):
    return jnp.sum(lax.all_to_all(x, axis, 0, 0, tiled=True, axis_index_groups=groups), axis=0)


def share(x, groups):
    return sum_over(jnp.broadcast_to(x, (len(groups[0]), *x.shape)), "dp", groups)


PLANE_GROUPS = [[z * 8 + i for i in range(8)] for z in range(4)]
COLUMN_GROUPS = [[z * 8 + i for z in range(4)] for i in range(8)]


def after(x, earlier):
    return lax.optimization_barrier((x, earlier))


def shards(grad_partials, momentum, params, kept):
    grad = grad_partials[0, 0]
    rest1, sent1 = first_of(kept, grad)
    rest2, sent2 = second_of(grad)
    state_coef, reject, expand = state_of(kept, momentum)

    got1 = halve(sent1, 0, "y")
    got2 = halve(sent2, 0, "y")
    next1 = rest1[1] + got1[1]
    last1 = halve(next1, 1, "y")
    got2, _ = after(got2, next1)
    last2 = halve(rest2[1] + got2[1], 1, "y")

    sum1 = rest1[0] + got1[0] + last1
    got1 = halve(sum1[2:], 0, "z")
    last2, _ = after(last2, sum1)
    sum2 = rest2[0] + got2[0] + last2
    got2 = halve(sum2[2:], 0, "z")
    next1 = sum1[1] + got1[1]
    last1 = halve(next1, 1, "z")
    own1 = sum1[0] + got1[0]

    coef = own1[:, :COEFFS] + last1[:, :COEFFS] + state_coef
    coef = share(coef, PLANE_GROUPS)
    got2, coef = after(got2, coef)
    last2 = halve(sum2[1] + got2[1], 1, "z")
    own2 = sum2[0] + got2[0]
    coef = share(coef, COLUMN_GROUPS)
    new_params = new_params_of(coef, params, expand)
    last2, new_params = after(last2, new_params)
    new_momentum = new_momentum_of((own1, last1), (own2, last2), momentum, reject)
    return (new_params, new_momentum)


def solution(mesh):
    placed = (
        P("dp", "fsdp", None, None, None),
        P("dp", None, "fsdp", None),
        P(None, "fsdp", None),
        P(),
    )
    return jax.shard_map(
        shards,
        mesh=mesh,
        in_specs=placed,
        out_specs=(P(None, "fsdp", None), P("dp", None, "fsdp", None)),
        check_vma=False,
    )
```

```python
import math

import jax
import jax.numpy as jnp
import numpy as np
from jax import lax
from jax.experimental import pallas as pl
from jax.experimental.pallas import tpu as pltpu
from jax.sharding import PartitionSpec as P

SPAN = 64
KEEP = 8
ROW_VALS = 5120
LAYERS = 2
GROUP = 128 // KEEP
WIDE = GROUP * SPAN
CHUNKS = ROW_VALS // WIDE
COEFFS = ROW_VALS // SPAN * KEEP
OWN = 8
HIGHEST = lax.Precision.HIGHEST
BOTH = ("dp", "fsdp")
N_DP = 32
N_FSDP = 16


def picked_t(kept_ref):
    lane = lax.broadcasted_iota(jnp.int32, (SPAN, 128), 1) % KEEP
    n = lax.broadcasted_iota(jnp.int32, (SPAN, 128), 0)
    k = jnp.zeros((SPAN, 128), jnp.int32)
    for j in range(KEEP):
        k = jnp.where(lane == j, kept_ref[j], k)
    turn = ((2 * n + 1) * k) & (4 * SPAN - 1)
    turn = jnp.minimum(turn, 4 * SPAN - turn)
    flip = turn > SPAN
    angle = jnp.where(flip, 2 * SPAN - turn, turn).astype(jnp.float32) * np.float32(np.pi / (2 * SPAN))
    square = angle * angle
    value = jnp.full((SPAN, 128), (-1.0) ** 8 / math.factorial(16), jnp.float32)
    for term in range(7, -1, -1):
        value = value * square + (-1.0) ** term / math.factorial(2 * term)
    value = jnp.where(flip, -value, value)
    return value * jnp.where(k == 0, np.float32(np.sqrt(1.0 / SPAN)), np.float32(np.sqrt(2.0 / SPAN)))


def spread(picked):
    tall = jnp.concatenate([picked] * GROUP, axis=0)
    row = lax.broadcasted_iota(jnp.int32, (WIDE, 128), 0)
    col = lax.broadcasted_iota(jnp.int32, (WIDE, 128), 1)
    return jnp.where(row // SPAN == col // KEEP, tall, 0.0)


def row_order(by_slot):
    y, z = lax.axis_index("fsdp") % 4, lax.axis_index("fsdp") // 4
    near = 1 + 2 * (lax.axis_index("dp") % 2)
    far = 4 - near
    r = lax.broadcasted_iota(jnp.int32, (128, 128), 0)
    col = lax.broadcasted_iota(jnp.int32, (128, 128), 1)

    def partner(slot):
        return jnp.where(slot == 0, 0, jnp.where(slot == 1, far, jnp.where(slot == 2, near, 2)))

    major, minor = r // (4 * OWN), (r // OWN) % 4
    to_y = y ^ partner(major) if by_slot else minor
    to_z = z ^ partner(minor if by_slot else major)
    source = ((r // 4) % 2) * 64 + to_z * 16 + to_y * 4 + r % 4
    return (source == col).astype(jnp.float32).astype(jnp.bfloat16)


def main_kernel(grad_ref, rest_ref, sent_ref):
    order = row_order(True)
    for c in range(CHUNKS):
        lanes = slice(c * WIDE, (c + 1) * WIDE)
        values = grad_ref[:, :, lanes].reshape(128, WIDE)
        rows = jnp.dot(order, values, preferred_element_type=jnp.float32)
        rest_ref[:, :, :, lanes] = rows[:64].reshape(2, 4, OWN, WIDE)
        sent_ref[:, :, :, lanes] = rows[64:].reshape(2, 4, OWN, WIDE)


def main_of(grad):
    vmem = pl.BlockSpec(memory_space=pltpu.VMEM)
    half = jax.ShapeDtypeStruct((2, 4, OWN, ROW_VALS), jnp.float32)
    return pl.pallas_call(
        main_kernel,
        out_shape=(half, half),
        in_specs=[vmem],
        out_specs=(vmem, vmem),
        compiler_params=pltpu.CompilerParams(vmem_limit_bytes=32 * 2**20),
        cost_estimate=pl.CostEstimate(flops=200_000_000, bytes_accessed=4_000_000, transcendentals=0),
        name="main",
    )(grad)


def coef_kernel(kept_ref, grad_ref, rest_ref, sent_ref):
    order = row_order(False)
    picked = picked_t(kept_ref)
    high = picked.astype(jnp.bfloat16).astype(jnp.float32)
    wide = jnp.concatenate([spread(high), spread(picked - high)], axis=1).astype(jnp.bfloat16)
    for c in range(CHUNKS):
        values = grad_ref[:, :, c * WIDE:(c + 1) * WIDE].reshape(128, WIDE)
        rows = jnp.dot(order, values, preferred_element_type=jnp.float32).astype(jnp.bfloat16)
        both = jnp.dot(rows, wide, preferred_element_type=jnp.float32)
        coef = both[:, :128] + both[:, 128:]
        lanes = slice(c * 128, (c + 1) * 128)
        rest_ref[:, :, :, lanes] = coef[:64].reshape(2, 4, OWN, 128)
        sent_ref[:, :, :, lanes] = coef[64:].reshape(2, 4, OWN, 128)


def coef_of(kept, grad):
    vmem = pl.BlockSpec(memory_space=pltpu.VMEM)
    half = jax.ShapeDtypeStruct((2, 4, OWN, COEFFS), jnp.float32)
    return pl.pallas_call(
        coef_kernel,
        out_shape=(half, half),
        in_specs=[pl.BlockSpec(memory_space=pltpu.SMEM), vmem],
        out_specs=(vmem, vmem),
        compiler_params=pltpu.CompilerParams(vmem_limit_bytes=32 * 2**20),
        cost_estimate=pl.CostEstimate(flops=500_000_000, bytes_accessed=2_000_000, transcendentals=0),
        name="coef",
    )(kept, grad)


def tall(x):
    return jnp.concatenate([x[:, c * 128:(c + 1) * 128] for c in range(x.shape[1] // 128)], axis=0)


def state_kernel(kept_ref, momentum_ref, coef_ref, reject_ref, expand_ref):
    wide = spread(picked_t(kept_ref))
    pair = wide[:128, :]
    row = lax.broadcasted_iota(jnp.int32, (128, 128), 0)
    col = lax.broadcasted_iota(jnp.int32, (128, 128), 1)
    onto = lax.dot_general(pair, pair, (((1,), (1,)), ((), ())), precision=HIGHEST, preferred_element_type=jnp.float32)
    reject_ref[...] = jnp.where(row == col, 1.0, 0.0) - onto
    expand_ref[...] = wide
    state = 0.9 * jnp.concatenate([momentum_ref[0, 0], momentum_ref[0, 1]], axis=0)
    deep = jnp.concatenate([state[:, c * WIDE:(c + 1) * WIDE] for c in range(CHUNKS)], axis=0)
    coef = jnp.dot(deep, wide, precision=HIGHEST, preferred_element_type=jnp.float32)
    for c in range(CHUNKS):
        coef_ref[:, c * 128:(c + 1) * 128] = coef[c * OWN:(c + 1) * OWN]


def state_of(kept, momentum):
    smem = pl.BlockSpec(memory_space=pltpu.SMEM)
    vmem = pl.BlockSpec(memory_space=pltpu.VMEM)
    return pl.pallas_call(
        state_kernel,
        out_shape=(
            jax.ShapeDtypeStruct((OWN, COEFFS), jnp.float32),
            jax.ShapeDtypeStruct((128, 128), jnp.float32),
            jax.ShapeDtypeStruct((WIDE, 128), jnp.float32),
        ),
        in_specs=[smem, vmem],
        out_specs=(vmem, vmem, vmem),
        compiler_params=pltpu.CompilerParams(vmem_limit_bytes=32 * 2**20),
        cost_estimate=pl.CostEstimate(flops=100_000_000, bytes_accessed=1_000_000, transcendentals=0),
        name="state",
    )(kept, momentum)


def momentum_kernel(own_ref, got_ref, momentum_ref, reject_ref, out_ref):
    state = jnp.concatenate([momentum_ref[0, 0], momentum_ref[0, 1]], axis=0)
    moment = 0.9 * state + (own_ref[...] + got_ref[...])
    new = jnp.dot(tall(moment), reject_ref[...], precision=HIGHEST, preferred_element_type=jnp.float32)
    for c in range(ROW_VALS // 128):
        part = new[c * OWN:(c + 1) * OWN]
        out_ref[0, 0, :, c * 128:(c + 1) * 128] = part[:4]
        out_ref[0, 1, :, c * 128:(c + 1) * 128] = part[4:]


def new_momentum_of(own, got, momentum, reject):
    vmem = pl.BlockSpec(memory_space=pltpu.VMEM)
    return pl.pallas_call(
        momentum_kernel,
        out_shape=jax.ShapeDtypeStruct(momentum.shape, jnp.float32),
        in_specs=[vmem] * 4,
        out_specs=vmem,
        compiler_params=pltpu.CompilerParams(vmem_limit_bytes=32 * 2**20),
        cost_estimate=pl.CostEstimate(flops=60_000_000, bytes_accessed=700_000, transcendentals=0),
        name="momentum",
    )(own, got, momentum, reject)


def params_kernel(total_ref, params_ref, expand_ref, out_ref):
    shared = total_ref[...] * (1.0 / N_DP)
    deep = tall(shared)
    update = lax.dot_general(
        deep, expand_ref[...], (((1,), (1,)), ((), ())), precision=HIGHEST, preferred_element_type=jnp.float32
    )
    for c in range(CHUNKS):
        lanes = slice(c * WIDE, (c + 1) * WIDE)
        part = update[c * OWN:(c + 1) * OWN]
        out_ref[0, :, lanes] = params_ref[0, :, lanes] - part[:4]
        out_ref[1, :, lanes] = params_ref[1, :, lanes] - part[4:]


def new_params_of(total, params, expand):
    vmem = pl.BlockSpec(memory_space=pltpu.VMEM)
    return pl.pallas_call(
        params_kernel,
        out_shape=jax.ShapeDtypeStruct(params.shape, jnp.float32),
        in_specs=[vmem] * 3,
        out_specs=vmem,
        compiler_params=pltpu.CompilerParams(vmem_limit_bytes=32 * 2**20),
        cost_estimate=pl.CostEstimate(flops=60_000_000, bytes_accessed=700_000, transcendentals=0),
        name="params",
    )(total, params, expand)


def sum_pairs(step, axis):
    pairs = []
    for d in range(N_DP):
        flip = (1, 3)[(d % 2) ^ step]
        for f in range(N_FSDP):
            to = f ^ (flip if axis == "y" else 4 * flip)
            pairs.append((d * N_FSDP + f, d * N_FSDP + to))
    return pairs


def halve(x, step, axis):
    return lax.ppermute(x, BOTH, sum_pairs(step, axis))


def sum_over(x, axis, groups):
    return jnp.sum(lax.all_to_all(x, axis, 0, 0, tiled=True, axis_index_groups=groups), axis=0)


def share(x, groups):
    return sum_over(jnp.broadcast_to(x, (len(groups[0]), *x.shape)), "dp", groups)


Y_GROUPS = [[z * 4 + y for y in range(4)] for z in range(4)]
PLANE_GROUPS = [[z * 8 + i for i in range(8)] for z in range(4)]
COLUMN_GROUPS = [[z * 8 + i for z in range(4)] for i in range(8)]


def after(x, earlier):
    return lax.optimization_barrier((x, earlier))


def shards(grad_partials, momentum, params, kept):
    grad = grad_partials[0, 0]
    main, sent = main_of(grad)
    got = halve(sent, 0, "y")
    coef, coef_sent = coef_of(kept, grad)
    state_coef, reject, expand = state_of(kept, momentum)

    coef_got = halve(coef_sent, 0, "z")
    coef_next = coef[1] + coef_got[1]
    got, coef_next = after(got, coef_next)
    last = halve(main[1] + got[1], 1, "y")

    coef_last = halve(coef_next, 1, "z")
    coef = coef[0] + coef_got[0] + coef_last
    last, coef = after(last, coef)
    main = main[0] + got[0] + last
    got = halve(main[2:], 0, "z")

    coef = sum_over(coef, "fsdp", Y_GROUPS) + state_coef
    coef = share(coef, COLUMN_GROUPS)
    got, coef = after(got, coef)
    last = halve(main[1] + got[1], 1, "z")

    coef = share(coef, PLANE_GROUPS)
    new_params = new_params_of(coef, params, expand)
    last, new_params = after(last, new_params)
    new_momentum = new_momentum_of(main[0] + got[0], last, momentum, reject)
    return (new_params, new_momentum)


def solution(mesh):
    placed = (
        P("dp", "fsdp", None, None, None),
        P("dp", None, "fsdp", None),
        P(None, "fsdp", None),
        P(),
    )
    return jax.shard_map(
        shards,
        mesh=mesh,
        in_specs=placed,
        out_specs=(P(None, "fsdp", None), P("dp", None, "fsdp", None)),
        check_vma=False,
    )
```

```python
import math

import jax
import jax.numpy as jnp
import numpy as np
from jax import lax
from jax.experimental import pallas as pl
from jax.experimental.pallas import tpu as pltpu
from jax.sharding import PartitionSpec as P

SPAN = 64
KEEP = 8
ROW_VALS = 5120
LAYERS = 2
GROUP = 128 // KEEP
WIDE = GROUP * SPAN
CHUNKS = ROW_VALS // WIDE
COEFFS = ROW_VALS // SPAN * KEEP
OWN = 8
HIGHEST = lax.Precision.HIGHEST
BOTH = ("dp", "fsdp")
N_DP = 32
N_FSDP = 16


def picked_t(kept_ref):
    lane = lax.broadcasted_iota(jnp.int32, (SPAN, 128), 1) % KEEP
    n = lax.broadcasted_iota(jnp.int32, (SPAN, 128), 0)
    k = jnp.zeros((SPAN, 128), jnp.int32)
    for j in range(KEEP):
        k = jnp.where(lane == j, kept_ref[j], k)
    turn = ((2 * n + 1) * k) & (4 * SPAN - 1)
    turn = jnp.minimum(turn, 4 * SPAN - turn)
    flip = turn > SPAN
    angle = jnp.where(flip, 2 * SPAN - turn, turn).astype(jnp.float32) * np.float32(np.pi / (2 * SPAN))
    square = angle * angle
    value = jnp.full((SPAN, 128), (-1.0) ** 8 / math.factorial(16), jnp.float32)
    for term in range(7, -1, -1):
        value = value * square + (-1.0) ** term / math.factorial(2 * term)
    value = jnp.where(flip, -value, value)
    return value * jnp.where(k == 0, np.float32(np.sqrt(1.0 / SPAN)), np.float32(np.sqrt(2.0 / SPAN)))


def spread(picked):
    tall = jnp.concatenate([picked] * GROUP, axis=0)
    row = lax.broadcasted_iota(jnp.int32, (WIDE, 128), 0)
    col = lax.broadcasted_iota(jnp.int32, (WIDE, 128), 1)
    return jnp.where(row // SPAN == col // KEEP, tall, 0.0)


def row_order(by_slot):
    y, z = lax.axis_index("fsdp") % 4, lax.axis_index("fsdp") // 4
    near = 1 + 2 * (lax.axis_index("dp") % 2)
    far = 4 - near
    r = lax.broadcasted_iota(jnp.int32, (128, 128), 0)
    col = lax.broadcasted_iota(jnp.int32, (128, 128), 1)

    def partner(slot):
        return jnp.where(slot == 0, 0, jnp.where(slot == 1, far, jnp.where(slot == 2, near, 2)))

    major, minor = r // (4 * OWN), (r // OWN) % 4
    to_y = y ^ partner(major) if by_slot else minor
    to_z = z ^ partner(minor if by_slot else major)
    source = ((r // 4) % 2) * 64 + to_z * 16 + to_y * 4 + r % 4
    return (source == col).astype(jnp.float32).astype(jnp.bfloat16)


def main_kernel(grad_ref, rest_ref, near_ref, across_ref):
    order = row_order(True)
    for c in range(CHUNKS):
        lanes = slice(c * WIDE, (c + 1) * WIDE)
        values = grad_ref[:, :, lanes].reshape(128, WIDE)
        rows = jnp.dot(order, values, preferred_element_type=jnp.float32)
        rest_ref[:, :, :, lanes] = rows[:64].reshape(2, 4, OWN, WIDE)
        near_ref[:, :, lanes] = rows[64:96].reshape(4, OWN, WIDE)
        across_ref[:, :, lanes] = rows[96:].reshape(4, OWN, WIDE)


def main_of(grad):
    vmem = pl.BlockSpec(memory_space=pltpu.VMEM)
    half = jax.ShapeDtypeStruct((2, 4, OWN, ROW_VALS), jnp.float32)
    quarter = jax.ShapeDtypeStruct((4, OWN, ROW_VALS), jnp.float32)
    return pl.pallas_call(
        main_kernel,
        out_shape=(half, quarter, quarter),
        in_specs=[vmem],
        out_specs=(vmem, vmem, vmem),
        compiler_params=pltpu.CompilerParams(vmem_limit_bytes=32 * 2**20),
        cost_estimate=pl.CostEstimate(flops=200_000_000, bytes_accessed=4_000_000, transcendentals=0),
        name="main",
    )(grad)


def coef_kernel(kept_ref, grad_ref, rest_ref, sent_ref):
    order = row_order(False)
    picked = picked_t(kept_ref)
    high = picked.astype(jnp.bfloat16).astype(jnp.float32)
    wide = jnp.concatenate([spread(high), spread(picked - high)], axis=1).astype(jnp.bfloat16)
    for c in range(CHUNKS):
        values = grad_ref[:, :, c * WIDE:(c + 1) * WIDE].reshape(128, WIDE)
        rows = jnp.dot(order, values, preferred_element_type=jnp.float32).astype(jnp.bfloat16)
        both = jnp.dot(rows, wide, preferred_element_type=jnp.float32)
        coef = both[:, :128] + both[:, 128:]
        lanes = slice(c * 128, (c + 1) * 128)
        rest_ref[:, :, :, lanes] = coef[:64].reshape(2, 4, OWN, 128)
        sent_ref[:, :, :, lanes] = coef[64:].reshape(2, 4, OWN, 128)


def coef_of(kept, grad):
    vmem = pl.BlockSpec(memory_space=pltpu.VMEM)
    half = jax.ShapeDtypeStruct((2, 4, OWN, COEFFS), jnp.float32)
    return pl.pallas_call(
        coef_kernel,
        out_shape=(half, half),
        in_specs=[pl.BlockSpec(memory_space=pltpu.SMEM), vmem],
        out_specs=(vmem, vmem),
        compiler_params=pltpu.CompilerParams(vmem_limit_bytes=32 * 2**20),
        cost_estimate=pl.CostEstimate(flops=500_000_000, bytes_accessed=2_000_000, transcendentals=0),
        name="coef",
    )(kept, grad)


def tall(x):
    return jnp.concatenate([x[:, c * 128:(c + 1) * 128] for c in range(x.shape[1] // 128)], axis=0)


def state_kernel(kept_ref, momentum_ref, coef_ref, reject_ref, expand_ref):
    wide = spread(picked_t(kept_ref))
    pair = wide[:128, :]
    row = lax.broadcasted_iota(jnp.int32, (128, 128), 0)
    col = lax.broadcasted_iota(jnp.int32, (128, 128), 1)
    onto = lax.dot_general(pair, pair, (((1,), (1,)), ((), ())), precision=HIGHEST, preferred_element_type=jnp.float32)
    reject_ref[...] = jnp.where(row == col, 1.0, 0.0) - onto
    expand_ref[...] = wide
    state = 0.9 * jnp.concatenate([momentum_ref[0, 0], momentum_ref[0, 1]], axis=0)
    deep = jnp.concatenate([state[:, c * WIDE:(c + 1) * WIDE] for c in range(CHUNKS)], axis=0)
    coef = jnp.dot(deep, wide, precision=HIGHEST, preferred_element_type=jnp.float32)
    for c in range(CHUNKS):
        coef_ref[:, c * 128:(c + 1) * 128] = coef[c * OWN:(c + 1) * OWN]


def state_of(kept, momentum):
    smem = pl.BlockSpec(memory_space=pltpu.SMEM)
    vmem = pl.BlockSpec(memory_space=pltpu.VMEM)
    return pl.pallas_call(
        state_kernel,
        out_shape=(
            jax.ShapeDtypeStruct((OWN, COEFFS), jnp.float32),
            jax.ShapeDtypeStruct((128, 128), jnp.float32),
            jax.ShapeDtypeStruct((WIDE, 128), jnp.float32),
        ),
        in_specs=[smem, vmem],
        out_specs=(vmem, vmem, vmem),
        compiler_params=pltpu.CompilerParams(vmem_limit_bytes=32 * 2**20),
        cost_estimate=pl.CostEstimate(flops=100_000_000, bytes_accessed=1_000_000, transcendentals=0),
        name="state",
    )(kept, momentum)


def momentum_kernel(own_ref, got_ref, momentum_ref, reject_ref, out_ref):
    state = jnp.concatenate([momentum_ref[0, 0], momentum_ref[0, 1]], axis=0)
    moment = 0.9 * state + (own_ref[...] + got_ref[...])
    new = jnp.dot(tall(moment), reject_ref[...], precision=HIGHEST, preferred_element_type=jnp.float32)
    for c in range(ROW_VALS // 128):
        part = new[c * OWN:(c + 1) * OWN]
        out_ref[0, 0, :, c * 128:(c + 1) * 128] = part[:4]
        out_ref[0, 1, :, c * 128:(c + 1) * 128] = part[4:]


def new_momentum_of(own, got, momentum, reject):
    vmem = pl.BlockSpec(memory_space=pltpu.VMEM)
    return pl.pallas_call(
        momentum_kernel,
        out_shape=jax.ShapeDtypeStruct(momentum.shape, jnp.float32),
        in_specs=[vmem] * 4,
        out_specs=vmem,
        compiler_params=pltpu.CompilerParams(vmem_limit_bytes=32 * 2**20),
        cost_estimate=pl.CostEstimate(flops=60_000_000, bytes_accessed=700_000, transcendentals=0),
        name="momentum",
    )(own, got, momentum, reject)


def params_kernel(parts_ref, params_ref, expand_ref, out_ref):
    shared = jnp.sum(parts_ref[...], axis=0) * (1.0 / N_DP)
    deep = tall(shared)
    update = lax.dot_general(
        deep, expand_ref[...], (((1,), (1,)), ((), ())), precision=HIGHEST, preferred_element_type=jnp.float32
    )
    for c in range(CHUNKS):
        lanes = slice(c * WIDE, (c + 1) * WIDE)
        part = update[c * OWN:(c + 1) * OWN]
        out_ref[0, :, lanes] = params_ref[0, :, lanes] - part[:4]
        out_ref[1, :, lanes] = params_ref[1, :, lanes] - part[4:]


def new_params_of(parts, params, expand):
    vmem = pl.BlockSpec(memory_space=pltpu.VMEM)
    return pl.pallas_call(
        params_kernel,
        out_shape=jax.ShapeDtypeStruct(params.shape, jnp.float32),
        in_specs=[vmem] * 3,
        out_specs=vmem,
        compiler_params=pltpu.CompilerParams(vmem_limit_bytes=32 * 2**20),
        cost_estimate=pl.CostEstimate(flops=60_000_000, bytes_accessed=700_000, transcendentals=0),
        name="params",
    )(parts, params, expand)


def sum_pairs(step, axis):
    pairs = []
    for d in range(N_DP):
        flip = (1, 3)[(d % 2) ^ step]
        for f in range(N_FSDP):
            to = f ^ (flip if axis == "y" else 4 * flip)
            pairs.append((d * N_FSDP + f, d * N_FSDP + to))
    return pairs


def halve(x, step, axis):
    return lax.ppermute(x, BOTH, sum_pairs(step, axis))


def deal(x, axis, groups):
    return lax.all_to_all(x, axis, 0, 0, tiled=True, axis_index_groups=groups)


def share_parts(x, groups):
    return deal(jnp.broadcast_to(x, (len(groups[0]), *x.shape)), "dp", groups)


def sum_over(x, axis, groups):
    return jnp.sum(lax.all_to_all(x, axis, 0, 0, tiled=True, axis_index_groups=groups), axis=0)


def share(x, groups):
    return sum_over(jnp.broadcast_to(x, (len(groups[0]), *x.shape)), "dp", groups)


Y_GROUPS = [[z * 4 + y for y in range(4)] for z in range(4)]
PLANE_GROUPS = [[z * 8 + i for i in range(8)] for z in range(4)]
COLUMN_GROUPS = [[z * 8 + i for z in range(4)] for i in range(8)]


def after(x, earlier):
    return lax.optimization_barrier((x, earlier))


def shards(grad_partials, momentum, params, kept):
    grad = grad_partials[0, 0]
    main, near, across = main_of(grad)
    across = halve(across, 0, "y")
    near = halve(near, 0, "y")
    coef, coef_sent = coef_of(kept, grad)
    state_coef, reject, expand = state_of(kept, momentum)

    coef_got = halve(coef_sent, 0, "z")
    coef_next = coef[1] + coef_got[1]
    across, coef_sent, state_coef = lax.optimization_barrier((across, coef_sent, state_coef))
    last = halve(main[1] + across, 1, "y")
    coef_last = halve(coef_next, 1, "z")
    coef = coef[0] + coef_got[0] + coef_last
    last, coef = after(last, coef)
    main = main[0] + near + last
    across = halve(main[3], 0, "z")
    near = halve(main[2], 0, "z")

    coef = sum_over(coef, "fsdp", Y_GROUPS) + state_coef
    across, coef = after(across, coef)
    last = halve(main[1] + across, 1, "z")
    coef = share(coef, COLUMN_GROUPS)
    coef = share_parts(coef, PLANE_GROUPS)
    new_params = new_params_of(coef, params, expand)
    new_momentum = new_momentum_of(main[0] + near, last, momentum, reject)
    return (new_params, new_momentum)


def solution(mesh):
    placed = (
        P("dp", "fsdp", None, None, None),
        P("dp", None, "fsdp", None),
        P(None, "fsdp", None),
        P(),
    )
    return jax.shard_map(
        shards,
        mesh=mesh,
        in_specs=placed,
        out_specs=(P(None, "fsdp", None), P("dp", None, "fsdp", None)),
        check_vma=False,
    )
```

```python
import math

import jax
import jax.numpy as jnp
import numpy as np
from jax import lax
from jax.experimental import pallas as pl
from jax.experimental.pallas import tpu as pltpu
from jax.sharding import PartitionSpec as P

SPAN = 64
KEEP = 8
ROW_VALS = 5120
LAYERS = 2
GROUP = 128 // KEEP
WIDE = GROUP * SPAN
CHUNKS = ROW_VALS // WIDE
COEFFS = ROW_VALS // SPAN * KEEP
OWN = 8
HIGHEST = lax.Precision.HIGHEST
BOTH = ("dp", "fsdp")
N_DP = 32
N_FSDP = 16


def picked_t(kept_ref):
    lane = lax.broadcasted_iota(jnp.int32, (SPAN, 128), 1) % KEEP
    n = lax.broadcasted_iota(jnp.int32, (SPAN, 128), 0)
    k = jnp.zeros((SPAN, 128), jnp.int32)
    for j in range(KEEP):
        k = jnp.where(lane == j, kept_ref[j], k)
    turn = ((2 * n + 1) * k) & (4 * SPAN - 1)
    turn = jnp.minimum(turn, 4 * SPAN - turn)
    flip = turn > SPAN
    angle = jnp.where(flip, 2 * SPAN - turn, turn).astype(jnp.float32) * np.float32(np.pi / (2 * SPAN))
    square = angle * angle
    value = jnp.full((SPAN, 128), (-1.0) ** 8 / math.factorial(16), jnp.float32)
    for term in range(7, -1, -1):
        value = value * square + (-1.0) ** term / math.factorial(2 * term)
    value = jnp.where(flip, -value, value)
    return value * jnp.where(k == 0, np.float32(np.sqrt(1.0 / SPAN)), np.float32(np.sqrt(2.0 / SPAN)))


def spread(picked):
    tall = jnp.concatenate([picked] * GROUP, axis=0)
    row = lax.broadcasted_iota(jnp.int32, (WIDE, 128), 0)
    col = lax.broadcasted_iota(jnp.int32, (WIDE, 128), 1)
    return jnp.where(row // SPAN == col // KEEP, tall, 0.0)


def row_order(by_slot):
    y, z = lax.axis_index("fsdp") % 4, lax.axis_index("fsdp") // 4
    near = 1 + 2 * (lax.axis_index("dp") % 2)
    far = 4 - near
    r = lax.broadcasted_iota(jnp.int32, (128, 128), 0)
    col = lax.broadcasted_iota(jnp.int32, (128, 128), 1)

    def partner(slot):
        return jnp.where(slot == 0, 0, jnp.where(slot == 1, far, jnp.where(slot == 2, near, 2)))

    major, minor = r // (4 * OWN), (r // OWN) % 4
    to_y = y ^ partner(major) if by_slot else minor
    to_z = z ^ partner(minor if by_slot else major)
    source = ((r // 4) % 2) * 64 + to_z * 16 + to_y * 4 + r % 4
    return (source == col).astype(jnp.float32).astype(jnp.bfloat16)


def main_kernel(grad_ref, rest_ref, near_ref, across_ref):
    order = row_order(True)
    for c in range(CHUNKS):
        lanes = slice(c * WIDE, (c + 1) * WIDE)
        values = grad_ref[:, :, lanes].reshape(128, WIDE)
        rows = jnp.dot(order, values, preferred_element_type=jnp.float32)
        rest_ref[:, :, :, lanes] = rows[:64].reshape(2, 4, OWN, WIDE)
        near_ref[:, :, lanes] = rows[64:96].reshape(4, OWN, WIDE)
        across_ref[:, :, lanes] = rows[96:].reshape(4, OWN, WIDE)


def main_of(grad):
    vmem = pl.BlockSpec(memory_space=pltpu.VMEM)
    half = jax.ShapeDtypeStruct((2, 4, OWN, ROW_VALS), jnp.float32)
    quarter = jax.ShapeDtypeStruct((4, OWN, ROW_VALS), jnp.float32)
    return pl.pallas_call(
        main_kernel,
        out_shape=(half, quarter, quarter),
        in_specs=[vmem],
        out_specs=(vmem, vmem, vmem),
        compiler_params=pltpu.CompilerParams(vmem_limit_bytes=32 * 2**20),
        cost_estimate=pl.CostEstimate(flops=200_000_000, bytes_accessed=4_000_000, transcendentals=0),
        name="main",
    )(grad)


def coef_kernel(kept_ref, grad_ref, rest_ref, sent_ref):
    order = row_order(False)
    picked = picked_t(kept_ref)
    high = picked.astype(jnp.bfloat16).astype(jnp.float32)
    wide = jnp.concatenate([spread(high), spread(picked - high)], axis=1).astype(jnp.bfloat16)
    rows = []
    for c in range(CHUNKS):
        values = grad_ref[:, :, c * WIDE:(c + 1) * WIDE].reshape(128, WIDE)
        rows.append(jnp.dot(order, values, preferred_element_type=jnp.float32).astype(jnp.bfloat16))
    both = jnp.dot(jnp.concatenate(rows, axis=0), wide, preferred_element_type=jnp.float32)
    for c in range(CHUNKS):
        coef = both[c * 128:(c + 1) * 128, :128] + both[c * 128:(c + 1) * 128, 128:]
        lanes = slice(c * 128, (c + 1) * 128)
        rest_ref[:, :, :, lanes] = coef[:64].reshape(2, 4, OWN, 128)
        sent_ref[:, :, :, lanes] = coef[64:].reshape(2, 4, OWN, 128)


def coef_of(kept, grad):
    vmem = pl.BlockSpec(memory_space=pltpu.VMEM)
    half = jax.ShapeDtypeStruct((2, 4, OWN, COEFFS), jnp.float32)
    return pl.pallas_call(
        coef_kernel,
        out_shape=(half, half),
        in_specs=[pl.BlockSpec(memory_space=pltpu.SMEM), vmem],
        out_specs=(vmem, vmem),
        compiler_params=pltpu.CompilerParams(vmem_limit_bytes=32 * 2**20),
        cost_estimate=pl.CostEstimate(flops=500_000_000, bytes_accessed=2_000_000, transcendentals=0),
        name="coef",
    )(kept, grad)


def tall(x):
    return jnp.concatenate([x[:, c * 128:(c + 1) * 128] for c in range(x.shape[1] // 128)], axis=0)


def state_kernel(kept_ref, momentum_ref, coef_ref, reject_ref, expand_ref, rest_ref):
    wide = spread(picked_t(kept_ref))
    pair = wide[:128, :]
    row = lax.broadcasted_iota(jnp.int32, (128, 128), 0)
    col = lax.broadcasted_iota(jnp.int32, (128, 128), 1)
    onto = lax.dot_general(pair, pair, (((1,), (1,)), ((), ())), precision=HIGHEST, preferred_element_type=jnp.float32)
    reject_ref[...] = jnp.where(row == col, 1.0, 0.0) - onto
    across = wide.T
    high = across.astype(jnp.bfloat16)
    expand_ref[...] = high
    rest_ref[...] = (across - high.astype(jnp.float32)).astype(jnp.bfloat16)
    state = 0.9 * jnp.concatenate([momentum_ref[0, 0], momentum_ref[0, 1]], axis=0)
    deep = jnp.concatenate([state[:, c * WIDE:(c + 1) * WIDE] for c in range(CHUNKS)], axis=0)
    coef = jnp.dot(deep, wide, precision=HIGHEST, preferred_element_type=jnp.float32)
    for c in range(CHUNKS):
        coef_ref[:, c * 128:(c + 1) * 128] = coef[c * OWN:(c + 1) * OWN]


def state_of(kept, momentum):
    smem = pl.BlockSpec(memory_space=pltpu.SMEM)
    vmem = pl.BlockSpec(memory_space=pltpu.VMEM)
    return pl.pallas_call(
        state_kernel,
        out_shape=(
            jax.ShapeDtypeStruct((OWN, COEFFS), jnp.float32),
            jax.ShapeDtypeStruct((128, 128), jnp.float32),
            jax.ShapeDtypeStruct((128, WIDE), jnp.bfloat16),
            jax.ShapeDtypeStruct((128, WIDE), jnp.bfloat16),
        ),
        in_specs=[smem, vmem],
        out_specs=(vmem, vmem, vmem, vmem),
        compiler_params=pltpu.CompilerParams(vmem_limit_bytes=32 * 2**20),
        cost_estimate=pl.CostEstimate(flops=100_000_000, bytes_accessed=1_000_000, transcendentals=0),
        name="state",
    )(kept, momentum)


def momentum_kernel(own_ref, got_ref, momentum_ref, reject_ref, out_ref):
    state = jnp.concatenate([momentum_ref[0, 0], momentum_ref[0, 1]], axis=0)
    moment = 0.9 * state + (own_ref[...] + got_ref[...])
    new = jnp.dot(tall(moment), reject_ref[...], precision=HIGHEST, preferred_element_type=jnp.float32)
    for c in range(ROW_VALS // 128):
        part = new[c * OWN:(c + 1) * OWN]
        out_ref[0, 0, :, c * 128:(c + 1) * 128] = part[:4]
        out_ref[0, 1, :, c * 128:(c + 1) * 128] = part[4:]


def new_momentum_of(own, got, momentum, reject):
    vmem = pl.BlockSpec(memory_space=pltpu.VMEM)
    return pl.pallas_call(
        momentum_kernel,
        out_shape=jax.ShapeDtypeStruct(momentum.shape, jnp.float32),
        in_specs=[vmem] * 4,
        out_specs=vmem,
        compiler_params=pltpu.CompilerParams(vmem_limit_bytes=32 * 2**20),
        cost_estimate=pl.CostEstimate(flops=60_000_000, bytes_accessed=700_000, transcendentals=0),
        name="momentum",
    )(own, got, momentum, reject)


def params_kernel(parts_ref, params_ref, expand_ref, rest_ref, out_ref):
    shared = jnp.sum(parts_ref[...], axis=0) * (1.0 / N_DP)
    deep = tall(shared)
    high = deep.astype(jnp.bfloat16)
    low = (deep - high.astype(jnp.float32)).astype(jnp.bfloat16)
    update = jnp.dot(jnp.concatenate([high, low], axis=0), expand_ref[...], preferred_element_type=jnp.float32)
    update = update[:CHUNKS * OWN] + update[CHUNKS * OWN:]
    update = update + jnp.dot(high, rest_ref[...], preferred_element_type=jnp.float32)
    for c in range(CHUNKS):
        lanes = slice(c * WIDE, (c + 1) * WIDE)
        part = update[c * OWN:(c + 1) * OWN]
        out_ref[0, :, lanes] = params_ref[0, :, lanes] - part[:4]
        out_ref[1, :, lanes] = params_ref[1, :, lanes] - part[4:]


def new_params_of(parts, params, expand, rest):
    vmem = pl.BlockSpec(memory_space=pltpu.VMEM)
    return pl.pallas_call(
        params_kernel,
        out_shape=jax.ShapeDtypeStruct(params.shape, jnp.float32),
        in_specs=[vmem] * 4,
        out_specs=vmem,
        compiler_params=pltpu.CompilerParams(vmem_limit_bytes=32 * 2**20),
        cost_estimate=pl.CostEstimate(flops=60_000_000, bytes_accessed=700_000, transcendentals=0),
        name="params",
    )(parts, params, expand, rest)


def sum_pairs(step, axis):
    pairs = []
    for d in range(N_DP):
        flip = (1, 3)[(d % 2) ^ step]
        for f in range(N_FSDP):
            to = f ^ (flip if axis == "y" else 4 * flip)
            pairs.append((d * N_FSDP + f, d * N_FSDP + to))
    return pairs


def halve(x, step, axis):
    return lax.ppermute(x, BOTH, sum_pairs(step, axis))


def deal(x, axis, groups):
    return lax.all_to_all(x, axis, 0, 0, tiled=True, axis_index_groups=groups)


def share_parts(x, groups):
    return deal(jnp.broadcast_to(x, (len(groups[0]), *x.shape)), "dp", groups)


def sum_over(x, axis, groups):
    return jnp.sum(lax.all_to_all(x, axis, 0, 0, tiled=True, axis_index_groups=groups), axis=0)


def share(x, groups):
    return sum_over(jnp.broadcast_to(x, (len(groups[0]), *x.shape)), "dp", groups)


Y_GROUPS = [[z * 4 + y for y in range(4)] for z in range(4)]
PLANE_GROUPS = [[z * 8 + i for i in range(8)] for z in range(4)]
COLUMN_GROUPS = [[z * 8 + i for z in range(4)] for i in range(8)]


def after(x, earlier):
    return lax.optimization_barrier((x, earlier))


def shards(grad_partials, momentum, params, kept):
    grad = grad_partials[0, 0]
    main, near, across = main_of(grad)
    across = halve(across, 0, "y")
    near = halve(near, 0, "y")
    coef, coef_sent = coef_of(kept, grad)
    state_coef, reject, expand, rest = state_of(kept, momentum)

    coef_got = halve(coef_sent, 0, "z")
    across, coef_sent, state_coef = lax.optimization_barrier((across, coef_sent, state_coef))
    last = halve(main[1] + across, 1, "y")
    coef_next = coef[1] + coef_got[1]
    coef_last = halve(coef_next, 1, "z")
    coef = coef[0] + coef_got[0] + coef_last
    last, coef = after(last, coef)
    main = main[0] + near + last
    got = halve(main[2:], 0, "z")

    coef = sum_over(coef, "fsdp", Y_GROUPS) + state_coef
    last = halve(main[1] + got[1], 1, "z")
    coef = share(coef, COLUMN_GROUPS)
    coef = share_parts(coef, PLANE_GROUPS)
    new_params = new_params_of(coef, params, expand, rest)
    new_momentum = new_momentum_of(main[0] + got[0], last, momentum, reject)
    return (new_params, new_momentum)


def solution(mesh):
    placed = (
        P("dp", "fsdp", None, None, None),
        P("dp", None, "fsdp", None),
        P(None, "fsdp", None),
        P(),
    )
    return jax.shard_map(
        shards,
        mesh=mesh,
        in_specs=placed,
        out_specs=(P(None, "fsdp", None), P("dp", None, "fsdp", None)),
        check_vma=False,
    )
```

```python
import math

import jax
import jax.numpy as jnp
import numpy as np
from jax import lax
from jax.experimental import pallas as pl
from jax.experimental.pallas import tpu as pltpu
from jax.sharding import PartitionSpec as P

SPAN = 64
KEEP = 8
ROW_VALS = 5120
LAYERS = 2
GROUP = 128 // KEEP
WIDE = GROUP * SPAN
CHUNKS = ROW_VALS // WIDE
COEFFS = ROW_VALS // SPAN * KEEP
OWN = 8
HIGHEST = lax.Precision.HIGHEST
BOTH = ("dp", "fsdp")
N_DP = 32
N_FSDP = 16


def picked_t(kept_ref):
    lane = lax.broadcasted_iota(jnp.int32, (SPAN, 128), 1) % KEEP
    n = lax.broadcasted_iota(jnp.int32, (SPAN, 128), 0)
    k = jnp.zeros((SPAN, 128), jnp.int32)
    for j in range(KEEP):
        k = jnp.where(lane == j, kept_ref[j], k)
    turn = ((2 * n + 1) * k) & (4 * SPAN - 1)
    turn = jnp.minimum(turn, 4 * SPAN - turn)
    flip = turn > SPAN
    angle = jnp.where(flip, 2 * SPAN - turn, turn).astype(jnp.float32) * np.float32(np.pi / (2 * SPAN))
    square = angle * angle
    value = jnp.full((SPAN, 128), (-1.0) ** 8 / math.factorial(16), jnp.float32)
    for term in range(7, -1, -1):
        value = value * square + (-1.0) ** term / math.factorial(2 * term)
    value = jnp.where(flip, -value, value)
    return value * jnp.where(k == 0, np.float32(np.sqrt(1.0 / SPAN)), np.float32(np.sqrt(2.0 / SPAN)))


def spread(picked):
    tall = jnp.concatenate([picked] * GROUP, axis=0)
    row = lax.broadcasted_iota(jnp.int32, (WIDE, 128), 0)
    col = lax.broadcasted_iota(jnp.int32, (WIDE, 128), 1)
    return jnp.where(row // SPAN == col // KEEP, tall, 0.0)


def row_order(by_slot):
    y, z = lax.axis_index("fsdp") % 4, lax.axis_index("fsdp") // 4
    near = 1 + 2 * (lax.axis_index("dp") % 2)
    far = 4 - near
    r = lax.broadcasted_iota(jnp.int32, (128, 128), 0)
    col = lax.broadcasted_iota(jnp.int32, (128, 128), 1)

    def partner(slot):
        return jnp.where(slot == 0, 0, jnp.where(slot == 1, far, jnp.where(slot == 2, near, 2)))

    major, minor = r // (4 * OWN), (r // OWN) % 4
    to_y = y ^ partner(major) if by_slot else minor
    to_z = z ^ partner(minor if by_slot else major)
    source = ((r // 4) % 2) * 64 + to_z * 16 + to_y * 4 + r % 4
    return (source == col).astype(jnp.float32).astype(jnp.bfloat16)


def main_kernel(grad_ref, rest_ref, near_ref, across_ref):
    order = row_order(True)
    for c in range(CHUNKS):
        lanes = slice(c * WIDE, (c + 1) * WIDE)
        values = grad_ref[:, :, lanes].reshape(128, WIDE)
        rows = jnp.dot(order, values, preferred_element_type=jnp.float32)
        rest_ref[:, :, :, lanes] = rows[:64].reshape(2, 4, OWN, WIDE)
        near_ref[:, :, lanes] = rows[64:96].reshape(4, OWN, WIDE)
        across_ref[:, :, lanes] = rows[96:].reshape(4, OWN, WIDE)


def main_of(grad):
    vmem = pl.BlockSpec(memory_space=pltpu.VMEM)
    half = jax.ShapeDtypeStruct((2, 4, OWN, ROW_VALS), jnp.float32)
    quarter = jax.ShapeDtypeStruct((4, OWN, ROW_VALS), jnp.float32)
    return pl.pallas_call(
        main_kernel,
        out_shape=(half, quarter, quarter),
        in_specs=[vmem],
        out_specs=(vmem, vmem, vmem),
        compiler_params=pltpu.CompilerParams(vmem_limit_bytes=32 * 2**20),
        cost_estimate=pl.CostEstimate(flops=200_000_000, bytes_accessed=4_000_000, transcendentals=0),
        name="main",
    )(grad)


def coef_kernel(kept_ref, grad_ref, rest_ref, sent_ref):
    order = row_order(False)
    picked = picked_t(kept_ref)
    high = picked.astype(jnp.bfloat16).astype(jnp.float32)
    wide = jnp.concatenate([spread(high), spread(picked - high)], axis=1).astype(jnp.bfloat16)
    rows = []
    for c in range(CHUNKS):
        values = grad_ref[:, :, c * WIDE:(c + 1) * WIDE].reshape(128, WIDE)
        rows.append(jnp.dot(order, values, preferred_element_type=jnp.float32).astype(jnp.bfloat16))
    both = jnp.dot(jnp.concatenate(rows, axis=0), wide, preferred_element_type=jnp.float32)
    for c in range(CHUNKS):
        coef = both[c * 128:(c + 1) * 128, :128] + both[c * 128:(c + 1) * 128, 128:]
        lanes = slice(c * 128, (c + 1) * 128)
        rest_ref[:, :, :, lanes] = coef[:64].reshape(2, 4, OWN, 128)
        sent_ref[:, :, :, lanes] = coef[64:].reshape(2, 4, OWN, 128)


def coef_of(kept, grad):
    vmem = pl.BlockSpec(memory_space=pltpu.VMEM)
    half = jax.ShapeDtypeStruct((2, 4, OWN, COEFFS), jnp.float32)
    return pl.pallas_call(
        coef_kernel,
        out_shape=(half, half),
        in_specs=[pl.BlockSpec(memory_space=pltpu.SMEM), vmem],
        out_specs=(vmem, vmem),
        compiler_params=pltpu.CompilerParams(vmem_limit_bytes=32 * 2**20),
        cost_estimate=pl.CostEstimate(flops=500_000_000, bytes_accessed=2_000_000, transcendentals=0),
        name="coef",
    )(kept, grad)


def tall(x):
    return jnp.concatenate([x[:, c * 128:(c + 1) * 128] for c in range(x.shape[1] // 128)], axis=0)


def state_kernel(kept_ref, momentum_ref, coef_ref, reject_ref, expand_ref, rest_ref):
    wide = spread(picked_t(kept_ref))
    pair = wide[:128, :]
    row = lax.broadcasted_iota(jnp.int32, (128, 128), 0)
    col = lax.broadcasted_iota(jnp.int32, (128, 128), 1)
    onto = lax.dot_general(pair, pair, (((1,), (1,)), ((), ())), precision=HIGHEST, preferred_element_type=jnp.float32)
    reject_ref[...] = jnp.where(row == col, 1.0, 0.0) - onto
    across = wide.T
    high = across.astype(jnp.bfloat16)
    expand_ref[...] = high
    rest_ref[...] = (across - high.astype(jnp.float32)).astype(jnp.bfloat16)
    state = 0.9 * jnp.concatenate([momentum_ref[0, 0], momentum_ref[0, 1]], axis=0)
    deep = jnp.concatenate([state[:, c * WIDE:(c + 1) * WIDE] for c in range(CHUNKS)], axis=0)
    coef = jnp.dot(deep, wide, precision=HIGHEST, preferred_element_type=jnp.float32)
    for c in range(CHUNKS):
        coef_ref[:, c * 128:(c + 1) * 128] = coef[c * OWN:(c + 1) * OWN]


def state_of(kept, momentum):
    smem = pl.BlockSpec(memory_space=pltpu.SMEM)
    vmem = pl.BlockSpec(memory_space=pltpu.VMEM)
    return pl.pallas_call(
        state_kernel,
        out_shape=(
            jax.ShapeDtypeStruct((OWN, COEFFS), jnp.float32),
            jax.ShapeDtypeStruct((128, 128), jnp.float32),
            jax.ShapeDtypeStruct((128, WIDE), jnp.bfloat16),
            jax.ShapeDtypeStruct((128, WIDE), jnp.bfloat16),
        ),
        in_specs=[smem, vmem],
        out_specs=(vmem, vmem, vmem, vmem),
        compiler_params=pltpu.CompilerParams(vmem_limit_bytes=32 * 2**20),
        cost_estimate=pl.CostEstimate(flops=100_000_000, bytes_accessed=1_000_000, transcendentals=0),
        name="state",
    )(kept, momentum)


def momentum_kernel(own_ref, got_ref, momentum_ref, reject_ref, out_ref):
    state = jnp.concatenate([momentum_ref[0, 0], momentum_ref[0, 1]], axis=0)
    moment = 0.9 * state + (own_ref[...] + got_ref[...])
    new = jnp.dot(tall(moment), reject_ref[...], precision=HIGHEST, preferred_element_type=jnp.float32)
    for c in range(ROW_VALS // 128):
        part = new[c * OWN:(c + 1) * OWN]
        out_ref[0, 0, :, c * 128:(c + 1) * 128] = part[:4]
        out_ref[0, 1, :, c * 128:(c + 1) * 128] = part[4:]


def new_momentum_of(own, got, momentum, reject):
    vmem = pl.BlockSpec(memory_space=pltpu.VMEM)
    return pl.pallas_call(
        momentum_kernel,
        out_shape=jax.ShapeDtypeStruct(momentum.shape, jnp.float32),
        in_specs=[vmem] * 4,
        out_specs=vmem,
        compiler_params=pltpu.CompilerParams(vmem_limit_bytes=32 * 2**20),
        cost_estimate=pl.CostEstimate(flops=60_000_000, bytes_accessed=700_000, transcendentals=0),
        name="momentum",
    )(own, got, momentum, reject)


def params_kernel(parts_ref, params_ref, expand_ref, rest_ref, out_ref):
    shared = jnp.sum(parts_ref[...], axis=0) * (1.0 / N_DP)
    deep = tall(shared)
    high = deep.astype(jnp.bfloat16)
    low = (deep - high.astype(jnp.float32)).astype(jnp.bfloat16)
    update = jnp.dot(jnp.concatenate([high, low], axis=0), expand_ref[...], preferred_element_type=jnp.float32)
    update = update[:CHUNKS * OWN] + update[CHUNKS * OWN:]
    update = update + jnp.dot(high, rest_ref[...], preferred_element_type=jnp.float32)
    for c in range(CHUNKS):
        lanes = slice(c * WIDE, (c + 1) * WIDE)
        part = update[c * OWN:(c + 1) * OWN]
        out_ref[0, :, lanes] = params_ref[0, :, lanes] - part[:4]
        out_ref[1, :, lanes] = params_ref[1, :, lanes] - part[4:]


def new_params_of(parts, params, expand, rest):
    vmem = pl.BlockSpec(memory_space=pltpu.VMEM)
    return pl.pallas_call(
        params_kernel,
        out_shape=jax.ShapeDtypeStruct(params.shape, jnp.float32),
        in_specs=[vmem] * 4,
        out_specs=vmem,
        compiler_params=pltpu.CompilerParams(vmem_limit_bytes=32 * 2**20),
        cost_estimate=pl.CostEstimate(flops=60_000_000, bytes_accessed=700_000, transcendentals=0),
        name="params",
    )(parts, params, expand, rest)


def sum_pairs(step, axis):
    pairs = []
    for d in range(N_DP):
        flip = (1, 3)[(d % 2) ^ step]
        for f in range(N_FSDP):
            to = f ^ (flip if axis == "y" else 4 * flip)
            pairs.append((d * N_FSDP + f, d * N_FSDP + to))
    return pairs


def halve(x, step, axis):
    return lax.ppermute(x, BOTH, sum_pairs(step, axis))


def deal(x, axis, groups):
    return lax.all_to_all(x, axis, 0, 0, tiled=True, axis_index_groups=groups)


def share_parts(x, groups):
    return deal(jnp.broadcast_to(x, (len(groups[0]), *x.shape)), "dp", groups)


def sum_over(x, axis, groups):
    return jnp.sum(lax.all_to_all(x, axis, 0, 0, tiled=True, axis_index_groups=groups), axis=0)


def share(x, groups):
    return sum_over(jnp.broadcast_to(x, (len(groups[0]), *x.shape)), "dp", groups)


Y_GROUPS = [[z * 4 + y for y in range(4)] for z in range(4)]
PLANE_GROUPS = [[z * 8 + x * 2 + c for x in range(4)] for z in range(4) for c in range(2)]
COLUMN_GROUPS = [[z * 8 + x * 2 + c for z in range(4) for c in range(2)] for x in range(4)]


def after(x, earlier):
    return lax.optimization_barrier((x, earlier))


def shards(grad_partials, momentum, params, kept):
    grad = grad_partials[0, 0]
    main, near, across = main_of(grad)
    across = halve(across, 0, "y")
    near = halve(near, 0, "y")
    coef, coef_sent = coef_of(kept, grad)
    state_coef, reject, expand, rest = state_of(kept, momentum)

    coef_got = halve(coef_sent, 0, "z")
    across, coef_sent, state_coef = lax.optimization_barrier((across, coef_sent, state_coef))
    last = halve(main[1] + across, 1, "y")
    coef_next = coef[1] + coef_got[1]
    coef_last = halve(coef_next, 1, "z")
    coef = coef[0] + coef_got[0] + coef_last
    last, coef = after(last, coef)
    main = main[0] + near + last
    got = halve(main[2:], 0, "z")

    coef = sum_over(coef, "fsdp", Y_GROUPS) + state_coef
    last = halve(main[1] + got[1], 1, "z")
    coef = share(coef, COLUMN_GROUPS)
    coef = share_parts(coef, PLANE_GROUPS)
    new_params = new_params_of(coef, params, expand, rest)
    new_momentum = new_momentum_of(main[0] + got[0], last, momentum, reject)
    return (new_params, new_momentum)


def solution(mesh):
    placed = (
        P("dp", "fsdp", None, None, None),
        P("dp", None, "fsdp", None),
        P(None, "fsdp", None),
        P(),
    )
    return jax.shard_map(
        shards,
        mesh=mesh,
        in_specs=placed,
        out_specs=(P(None, "fsdp", None), P("dp", None, "fsdp", None)),
        check_vma=False,
    )
```

```python
import math

import jax
import jax.numpy as jnp
import numpy as np
from jax import lax
from jax.experimental import pallas as pl
from jax.experimental.pallas import tpu as pltpu
from jax.sharding import PartitionSpec as P

SPAN = 64
KEEP = 8
ROW_VALS = 5120
LAYERS = 2
GROUP = 128 // KEEP
WIDE = GROUP * SPAN
CHUNKS = ROW_VALS // WIDE
COEFFS = ROW_VALS // SPAN * KEEP
OWN = 8
HIGHEST = lax.Precision.HIGHEST
BOTH = ("dp", "fsdp")
N_DP = 32
N_FSDP = 16


def picked_t(kept_ref):
    lane = lax.broadcasted_iota(jnp.int32, (SPAN, 128), 1) % KEEP
    n = lax.broadcasted_iota(jnp.int32, (SPAN, 128), 0)
    k = jnp.zeros((SPAN, 128), jnp.int32)
    for j in range(KEEP):
        k = jnp.where(lane == j, kept_ref[j], k)
    turn = ((2 * n + 1) * k) & (4 * SPAN - 1)
    turn = jnp.minimum(turn, 4 * SPAN - turn)
    flip = turn > SPAN
    angle = jnp.where(flip, 2 * SPAN - turn, turn).astype(jnp.float32) * np.float32(np.pi / (2 * SPAN))
    square = angle * angle
    value = jnp.full((SPAN, 128), (-1.0) ** 8 / math.factorial(16), jnp.float32)
    for term in range(7, -1, -1):
        value = value * square + (-1.0) ** term / math.factorial(2 * term)
    value = jnp.where(flip, -value, value)
    return value * jnp.where(k == 0, np.float32(np.sqrt(1.0 / SPAN)), np.float32(np.sqrt(2.0 / SPAN)))


def spread(picked):
    tall = jnp.concatenate([picked] * GROUP, axis=0)
    row = lax.broadcasted_iota(jnp.int32, (WIDE, 128), 0)
    col = lax.broadcasted_iota(jnp.int32, (WIDE, 128), 1)
    return jnp.where(row // SPAN == col // KEEP, tall, 0.0)


def row_order(by_slot):
    y, z = lax.axis_index("fsdp") % 4, lax.axis_index("fsdp") // 4
    near = 1 + 2 * (lax.axis_index("dp") % 2)
    far = 4 - near
    r = lax.broadcasted_iota(jnp.int32, (128, 128), 0)
    col = lax.broadcasted_iota(jnp.int32, (128, 128), 1)

    def partner(slot):
        return jnp.where(slot == 0, 0, jnp.where(slot == 1, far, jnp.where(slot == 2, near, 2)))

    major, minor = r // (4 * OWN), (r // OWN) % 4
    to_y = y ^ partner(major) if by_slot else minor
    to_z = z ^ partner(minor if by_slot else major)
    source = ((r // 4) % 2) * 64 + to_z * 16 + to_y * 4 + r % 4
    return (source == col).astype(jnp.float32).astype(jnp.bfloat16)


def main_kernel(grad_ref, rest_ref, near_ref, across_ref):
    order = row_order(True)
    for c in range(CHUNKS):
        lanes = slice(c * WIDE, (c + 1) * WIDE)
        values = grad_ref[:, :, lanes].reshape(128, WIDE)
        rows = jnp.dot(order, values, preferred_element_type=jnp.float32)
        rest_ref[:, :, :, lanes] = rows[:64].reshape(2, 4, OWN, WIDE)
        near_ref[:, :, lanes] = rows[64:96].reshape(4, OWN, WIDE)
        across_ref[:, :, lanes] = rows[96:].reshape(4, OWN, WIDE)


def main_of(grad):
    vmem = pl.BlockSpec(memory_space=pltpu.VMEM)
    half = jax.ShapeDtypeStruct((2, 4, OWN, ROW_VALS), jnp.float32)
    quarter = jax.ShapeDtypeStruct((4, OWN, ROW_VALS), jnp.float32)
    return pl.pallas_call(
        main_kernel,
        out_shape=(half, quarter, quarter),
        in_specs=[vmem],
        out_specs=(vmem, vmem, vmem),
        compiler_params=pltpu.CompilerParams(vmem_limit_bytes=32 * 2**20),
        cost_estimate=pl.CostEstimate(flops=200_000_000, bytes_accessed=4_000_000, transcendentals=0),
        name="main",
    )(grad)


def coef_kernel(kept_ref, grad_ref, rest_ref, sent_ref):
    order = row_order(False)
    picked = picked_t(kept_ref)
    high = picked.astype(jnp.bfloat16).astype(jnp.float32)
    wide = jnp.concatenate([spread(high), spread(picked - high)], axis=1).astype(jnp.bfloat16)
    rows = []
    for c in range(CHUNKS):
        values = grad_ref[:, :, c * WIDE:(c + 1) * WIDE].reshape(128, WIDE)
        rows.append(jnp.dot(order, values, preferred_element_type=jnp.float32).astype(jnp.bfloat16))
    both = jnp.dot(jnp.concatenate(rows, axis=0), wide, preferred_element_type=jnp.float32)
    for c in range(CHUNKS):
        coef = both[c * 128:(c + 1) * 128, :128] + both[c * 128:(c + 1) * 128, 128:]
        lanes = slice(c * 128, (c + 1) * 128)
        rest_ref[:, :, :, lanes] = coef[:64].reshape(2, 4, OWN, 128)
        sent_ref[:, :, :, lanes] = coef[64:].reshape(2, 4, OWN, 128)


def coef_of(kept, grad):
    vmem = pl.BlockSpec(memory_space=pltpu.VMEM)
    half = jax.ShapeDtypeStruct((2, 4, OWN, COEFFS), jnp.float32)
    return pl.pallas_call(
        coef_kernel,
        out_shape=(half, half),
        in_specs=[pl.BlockSpec(memory_space=pltpu.SMEM), vmem],
        out_specs=(vmem, vmem),
        compiler_params=pltpu.CompilerParams(vmem_limit_bytes=32 * 2**20),
        cost_estimate=pl.CostEstimate(flops=500_000_000, bytes_accessed=2_000_000, transcendentals=0),
        name="coef",
    )(kept, grad)


def tall(x):
    return jnp.concatenate([x[:, c * 128:(c + 1) * 128] for c in range(x.shape[1] // 128)], axis=0)


def state_kernel(kept_ref, momentum_ref, coef_ref, reject_ref, expand_ref, rest_ref):
    wide = spread(picked_t(kept_ref))
    pair = wide[:128, :]
    row = lax.broadcasted_iota(jnp.int32, (128, 128), 0)
    col = lax.broadcasted_iota(jnp.int32, (128, 128), 1)
    onto = lax.dot_general(pair, pair, (((1,), (1,)), ((), ())), precision=HIGHEST, preferred_element_type=jnp.float32)
    reject_ref[...] = jnp.where(row == col, 1.0, 0.0) - onto
    across = wide.T
    high = across.astype(jnp.bfloat16)
    expand_ref[...] = high
    rest_ref[...] = (across - high.astype(jnp.float32)).astype(jnp.bfloat16)
    state = 0.9 * jnp.concatenate([momentum_ref[0, 0], momentum_ref[0, 1]], axis=0)
    deep = jnp.concatenate([state[:, c * WIDE:(c + 1) * WIDE] for c in range(CHUNKS)], axis=0)
    coef = jnp.dot(deep, wide, precision=HIGHEST, preferred_element_type=jnp.float32)
    y = lax.axis_index("fsdp") % 4
    for c in range(CHUNKS):
        part = coef[c * OWN:(c + 1) * OWN]
        for slot in range(4):
            coef_ref[slot, :, c * 128:(c + 1) * 128] = jnp.where(slot == y, part, 0.0)


def state_of(kept, momentum):
    smem = pl.BlockSpec(memory_space=pltpu.SMEM)
    vmem = pl.BlockSpec(memory_space=pltpu.VMEM)
    return pl.pallas_call(
        state_kernel,
        out_shape=(
            jax.ShapeDtypeStruct((4, OWN, COEFFS), jnp.float32),
            jax.ShapeDtypeStruct((128, 128), jnp.float32),
            jax.ShapeDtypeStruct((128, WIDE), jnp.bfloat16),
            jax.ShapeDtypeStruct((128, WIDE), jnp.bfloat16),
        ),
        in_specs=[smem, vmem],
        out_specs=(vmem, vmem, vmem, vmem),
        compiler_params=pltpu.CompilerParams(vmem_limit_bytes=32 * 2**20),
        cost_estimate=pl.CostEstimate(flops=100_000_000, bytes_accessed=1_000_000, transcendentals=0),
        name="state",
    )(kept, momentum)


def momentum_kernel(own_ref, got_ref, momentum_ref, reject_ref, out_ref):
    state = jnp.concatenate([momentum_ref[0, 0], momentum_ref[0, 1]], axis=0)
    moment = 0.9 * state + (own_ref[...] + got_ref[...])
    new = jnp.dot(tall(moment), reject_ref[...], precision=HIGHEST, preferred_element_type=jnp.float32)
    for c in range(ROW_VALS // 128):
        part = new[c * OWN:(c + 1) * OWN]
        out_ref[0, 0, :, c * 128:(c + 1) * 128] = part[:4]
        out_ref[0, 1, :, c * 128:(c + 1) * 128] = part[4:]


def new_momentum_of(own, got, momentum, reject):
    vmem = pl.BlockSpec(memory_space=pltpu.VMEM)
    return pl.pallas_call(
        momentum_kernel,
        out_shape=jax.ShapeDtypeStruct(momentum.shape, jnp.float32),
        in_specs=[vmem] * 4,
        out_specs=vmem,
        compiler_params=pltpu.CompilerParams(vmem_limit_bytes=32 * 2**20),
        cost_estimate=pl.CostEstimate(flops=60_000_000, bytes_accessed=700_000, transcendentals=0),
        name="momentum",
    )(own, got, momentum, reject)


def params_kernel(parts_ref, params_ref, expand_ref, rest_ref, out_ref):
    shared = jnp.sum(parts_ref[...], axis=0) * (1.0 / N_DP)
    deep = tall(shared)
    high = deep.astype(jnp.bfloat16)
    low = (deep - high.astype(jnp.float32)).astype(jnp.bfloat16)
    update = jnp.dot(jnp.concatenate([high, low], axis=0), expand_ref[...], preferred_element_type=jnp.float32)
    update = update[:CHUNKS * OWN] + update[CHUNKS * OWN:]
    update = update + jnp.dot(high, rest_ref[...], preferred_element_type=jnp.float32)
    for c in range(CHUNKS):
        lanes = slice(c * WIDE, (c + 1) * WIDE)
        part = update[c * OWN:(c + 1) * OWN]
        out_ref[0, :, lanes] = params_ref[0, :, lanes] - part[:4]
        out_ref[1, :, lanes] = params_ref[1, :, lanes] - part[4:]


def new_params_of(parts, params, expand, rest):
    vmem = pl.BlockSpec(memory_space=pltpu.VMEM)
    return pl.pallas_call(
        params_kernel,
        out_shape=jax.ShapeDtypeStruct(params.shape, jnp.float32),
        in_specs=[vmem] * 4,
        out_specs=vmem,
        compiler_params=pltpu.CompilerParams(vmem_limit_bytes=32 * 2**20),
        cost_estimate=pl.CostEstimate(flops=60_000_000, bytes_accessed=700_000, transcendentals=0),
        name="params",
    )(parts, params, expand, rest)


def sum_pairs(step, axis):
    pairs = []
    for d in range(N_DP):
        flip = (1, 3)[(d % 2) ^ step]
        for f in range(N_FSDP):
            to = f ^ (flip if axis == "y" else 4 * flip)
            pairs.append((d * N_FSDP + f, d * N_FSDP + to))
    return pairs


def halve(x, step, axis):
    return lax.ppermute(x, BOTH, sum_pairs(step, axis))


def deal(x, axis, groups):
    return lax.all_to_all(x, axis, 0, 0, tiled=True, axis_index_groups=groups)


def share_parts(x, groups):
    return deal(jnp.broadcast_to(x, (len(groups[0]), *x.shape)), "dp", groups)


def sum_over(x, axis, groups):
    return jnp.sum(lax.all_to_all(x, axis, 0, 0, tiled=True, axis_index_groups=groups), axis=0)


def share(x, groups):
    return sum_over(jnp.broadcast_to(x, (len(groups[0]), *x.shape)), "dp", groups)


Y_GROUPS = [[z * 4 + y for y in range(4)] for z in range(4)]
PLANE_GROUPS = [[z * 8 + x * 2 + c for x in range(4)] for z in range(4) for c in range(2)]
COLUMN_GROUPS = [[z * 8 + i for z in range(4)] for i in range(8)]
PAIR_GROUPS = [
    [(lo * 8 + x * 2 + c) * N_FSDP + hi * 4 + y for c in range(2) for y in range(4)]
    for lo in range(4) for x in range(4) for hi in range(4)
]


def after(x, earlier):
    return lax.optimization_barrier((x, earlier))


def shards(grad_partials, momentum, params, kept):
    grad = grad_partials[0, 0]
    main, near, across = main_of(grad)
    across = halve(across, 0, "y")
    near = halve(near, 0, "y")
    coef, coef_sent = coef_of(kept, grad)
    state_coef, reject, expand, rest = state_of(kept, momentum)

    coef_got = halve(coef_sent, 0, "z")
    across, coef_sent, state_coef = lax.optimization_barrier((across, coef_sent, state_coef))
    last = halve(main[1] + across, 1, "y")
    coef_next = coef[1] + coef_got[1]
    coef_last = halve(coef_next, 1, "z")
    coef = coef[0] + coef_got[0] + coef_last
    last, coef = after(last, coef)
    main = main[0] + near + last
    got = halve(main[2:], 0, "z")

    coef = coef + state_coef
    coef = sum_over(jnp.broadcast_to(coef, (2, *coef.shape)).reshape(8, OWN, COEFFS), BOTH, PAIR_GROUPS)
    last = halve(main[1] + got[1], 1, "z")
    coef = share(coef, COLUMN_GROUPS)
    coef = share_parts(coef, PLANE_GROUPS)
    new_params = new_params_of(coef, params, expand, rest)
    new_momentum = new_momentum_of(main[0] + got[0], last, momentum, reject)
    return (new_params, new_momentum)


def solution(mesh):
    placed = (
        P("dp", "fsdp", None, None, None),
        P("dp", None, "fsdp", None),
        P(None, "fsdp", None),
        P(),
    )
    return jax.shard_map(
        shards,
        mesh=mesh,
        in_specs=placed,
        out_specs=(P(None, "fsdp", None), P("dp", None, "fsdp", None)),
        check_vma=False,
    )
```

```python
import math

import jax
import jax.numpy as jnp
import numpy as np
from jax import lax
from jax.experimental import pallas as pl
from jax.experimental.pallas import tpu as pltpu
from jax.sharding import PartitionSpec as P

SPAN = 64
KEEP = 8
ROW_VALS = 5120
LAYERS = 2
GROUP = 128 // KEEP
WIDE = GROUP * SPAN
CHUNKS = ROW_VALS // WIDE
COEFFS = ROW_VALS // SPAN * KEEP
OWN = 8
HIGHEST = lax.Precision.HIGHEST
BOTH = ("dp", "fsdp")
N_DP = 32
N_FSDP = 16


def picked_t(kept_ref):
    lane = lax.broadcasted_iota(jnp.int32, (SPAN, 128), 1) % KEEP
    n = lax.broadcasted_iota(jnp.int32, (SPAN, 128), 0)
    k = jnp.zeros((SPAN, 128), jnp.int32)
    for j in range(KEEP):
        k = jnp.where(lane == j, kept_ref[j], k)
    turn = ((2 * n + 1) * k) & (4 * SPAN - 1)
    turn = jnp.minimum(turn, 4 * SPAN - turn)
    flip = turn > SPAN
    angle = jnp.where(flip, 2 * SPAN - turn, turn).astype(jnp.float32) * np.float32(np.pi / (2 * SPAN))
    square = angle * angle
    value = jnp.full((SPAN, 128), (-1.0) ** 8 / math.factorial(16), jnp.float32)
    for term in range(7, -1, -1):
        value = value * square + (-1.0) ** term / math.factorial(2 * term)
    value = jnp.where(flip, -value, value)
    return value * jnp.where(k == 0, np.float32(np.sqrt(1.0 / SPAN)), np.float32(np.sqrt(2.0 / SPAN)))


def spread(picked):
    tall = jnp.concatenate([picked] * GROUP, axis=0)
    row = lax.broadcasted_iota(jnp.int32, (WIDE, 128), 0)
    col = lax.broadcasted_iota(jnp.int32, (WIDE, 128), 1)
    return jnp.where(row // SPAN == col // KEEP, tall, 0.0)


def row_order(by_slot):
    y, z = lax.axis_index("fsdp") % 4, lax.axis_index("fsdp") // 4
    near = 1 + 2 * (lax.axis_index("dp") % 2)
    far = 4 - near
    r = lax.broadcasted_iota(jnp.int32, (128, 128), 0)
    col = lax.broadcasted_iota(jnp.int32, (128, 128), 1)

    def partner(slot):
        return jnp.where(slot == 0, 0, jnp.where(slot == 1, far, jnp.where(slot == 2, near, 2)))

    major, minor = r // (4 * OWN), (r // OWN) % 4
    to_y = y ^ partner(major) if by_slot else minor
    to_z = z ^ partner(minor if by_slot else major)
    source = ((r // 4) % 2) * 64 + to_z * 16 + to_y * 4 + r % 4
    return (source == col).astype(jnp.float32).astype(jnp.bfloat16)


def main_kernel(grad_ref, rest_ref, near_ref, across_ref):
    order = row_order(True)
    for c in range(CHUNKS):
        lanes = slice(c * WIDE, (c + 1) * WIDE)
        values = grad_ref[:, :, lanes].reshape(128, WIDE)
        rows = jnp.dot(order, values, preferred_element_type=jnp.float32)
        rest_ref[:, :, :, lanes] = rows[:64].reshape(2, 4, OWN, WIDE)
        near_ref[:, :, lanes] = rows[64:96].reshape(4, OWN, WIDE)
        across_ref[:, :, lanes] = rows[96:].reshape(4, OWN, WIDE)


def main_of(grad):
    vmem = pl.BlockSpec(memory_space=pltpu.VMEM)
    half = jax.ShapeDtypeStruct((2, 4, OWN, ROW_VALS), jnp.float32)
    quarter = jax.ShapeDtypeStruct((4, OWN, ROW_VALS), jnp.float32)
    return pl.pallas_call(
        main_kernel,
        out_shape=(half, quarter, quarter),
        in_specs=[vmem],
        out_specs=(vmem, vmem, vmem),
        compiler_params=pltpu.CompilerParams(vmem_limit_bytes=32 * 2**20),
        cost_estimate=pl.CostEstimate(flops=200_000_000, bytes_accessed=4_000_000, transcendentals=0),
        name="main",
    )(grad)


def coef_kernel(kept_ref, grad_ref, rest_ref, sent_ref):
    order = row_order(False)
    picked = picked_t(kept_ref)
    high = picked.astype(jnp.bfloat16).astype(jnp.float32)
    wide = jnp.concatenate([spread(high), spread(picked - high)], axis=1).astype(jnp.bfloat16)
    rows = []
    for c in range(CHUNKS):
        values = grad_ref[:, :, c * WIDE:(c + 1) * WIDE].reshape(128, WIDE)
        rows.append(jnp.dot(order, values, preferred_element_type=jnp.float32).astype(jnp.bfloat16))
    both = jnp.dot(jnp.concatenate(rows, axis=0), wide, preferred_element_type=jnp.float32)
    for c in range(CHUNKS):
        coef = both[c * 128:(c + 1) * 128, :128] + both[c * 128:(c + 1) * 128, 128:]
        lanes = slice(c * 128, (c + 1) * 128)
        rest_ref[:, :, :, lanes] = coef[:64].reshape(2, 4, OWN, 128)
        sent_ref[:, :, :, lanes] = coef[64:].reshape(2, 4, OWN, 128)


def coef_of(kept, grad):
    vmem = pl.BlockSpec(memory_space=pltpu.VMEM)
    half = jax.ShapeDtypeStruct((2, 4, OWN, COEFFS), jnp.float32)
    return pl.pallas_call(
        coef_kernel,
        out_shape=(half, half),
        in_specs=[pl.BlockSpec(memory_space=pltpu.SMEM), vmem],
        out_specs=(vmem, vmem),
        compiler_params=pltpu.CompilerParams(vmem_limit_bytes=32 * 2**20),
        cost_estimate=pl.CostEstimate(flops=500_000_000, bytes_accessed=2_000_000, transcendentals=0),
        name="coef",
    )(kept, grad)


def tall(x):
    return jnp.concatenate([x[:, c * 128:(c + 1) * 128] for c in range(x.shape[1] // 128)], axis=0)


def state_kernel(kept_ref, momentum_ref, coef_ref, reject_ref, expand_ref, rest_ref):
    wide = spread(picked_t(kept_ref))
    pair = wide[:128, :]
    row = lax.broadcasted_iota(jnp.int32, (128, 128), 0)
    col = lax.broadcasted_iota(jnp.int32, (128, 128), 1)
    onto = lax.dot_general(pair, pair, (((1,), (1,)), ((), ())), precision=HIGHEST, preferred_element_type=jnp.float32)
    reject_ref[...] = jnp.where(row == col, 1.0, 0.0) - onto
    across = wide.T
    high = across.astype(jnp.bfloat16)
    expand_ref[...] = high
    rest_ref[...] = (across - high.astype(jnp.float32)).astype(jnp.bfloat16)
    state = 0.9 * jnp.concatenate([momentum_ref[0, 0], momentum_ref[0, 1]], axis=0)
    deep = jnp.concatenate([state[:, c * WIDE:(c + 1) * WIDE] for c in range(CHUNKS)], axis=0)
    coef = jnp.dot(deep, wide, precision=HIGHEST, preferred_element_type=jnp.float32)
    y = lax.axis_index("fsdp") % 4
    for c in range(CHUNKS):
        part = coef[c * OWN:(c + 1) * OWN]
        for slot in range(4):
            coef_ref[slot, :, c * 128:(c + 1) * 128] = jnp.where(slot == y, part, 0.0)


def state_of(kept, momentum):
    smem = pl.BlockSpec(memory_space=pltpu.SMEM)
    vmem = pl.BlockSpec(memory_space=pltpu.VMEM)
    return pl.pallas_call(
        state_kernel,
        out_shape=(
            jax.ShapeDtypeStruct((4, OWN, COEFFS), jnp.float32),
            jax.ShapeDtypeStruct((128, 128), jnp.float32),
            jax.ShapeDtypeStruct((128, WIDE), jnp.bfloat16),
            jax.ShapeDtypeStruct((128, WIDE), jnp.bfloat16),
        ),
        in_specs=[smem, vmem],
        out_specs=(vmem, vmem, vmem, vmem),
        compiler_params=pltpu.CompilerParams(vmem_limit_bytes=32 * 2**20),
        cost_estimate=pl.CostEstimate(flops=100_000_000, bytes_accessed=1_000_000, transcendentals=0),
        name="state",
    )(kept, momentum)


def momentum_kernel(own_ref, got_ref, momentum_ref, reject_ref, out_ref):
    state = jnp.concatenate([momentum_ref[0, 0], momentum_ref[0, 1]], axis=0)
    moment = 0.9 * state + (own_ref[...] + got_ref[...])
    new = jnp.dot(tall(moment), reject_ref[...], precision=HIGHEST, preferred_element_type=jnp.float32)
    for c in range(ROW_VALS // 128):
        part = new[c * OWN:(c + 1) * OWN]
        out_ref[0, 0, :, c * 128:(c + 1) * 128] = part[:4]
        out_ref[0, 1, :, c * 128:(c + 1) * 128] = part[4:]


def new_momentum_of(own, got, momentum, reject):
    vmem = pl.BlockSpec(memory_space=pltpu.VMEM)
    return pl.pallas_call(
        momentum_kernel,
        out_shape=jax.ShapeDtypeStruct(momentum.shape, jnp.float32),
        in_specs=[vmem] * 4,
        out_specs=vmem,
        compiler_params=pltpu.CompilerParams(vmem_limit_bytes=32 * 2**20),
        cost_estimate=pl.CostEstimate(flops=60_000_000, bytes_accessed=700_000, transcendentals=0),
        name="momentum",
    )(own, got, momentum, reject)


def params_kernel(parts_ref, params_ref, expand_ref, rest_ref, out_ref):
    shared = jnp.sum(parts_ref[...], axis=0) * (1.0 / N_DP)
    deep = tall(shared)
    high = deep.astype(jnp.bfloat16)
    low = (deep - high.astype(jnp.float32)).astype(jnp.bfloat16)
    update = jnp.dot(jnp.concatenate([high, low], axis=0), expand_ref[...], preferred_element_type=jnp.float32)
    update = update[:CHUNKS * OWN] + update[CHUNKS * OWN:]
    update = update + jnp.dot(high, rest_ref[...], preferred_element_type=jnp.float32)
    for c in range(CHUNKS):
        lanes = slice(c * WIDE, (c + 1) * WIDE)
        part = update[c * OWN:(c + 1) * OWN]
        out_ref[0, :, lanes] = params_ref[0, :, lanes] - part[:4]
        out_ref[1, :, lanes] = params_ref[1, :, lanes] - part[4:]


def new_params_of(parts, params, expand, rest):
    vmem = pl.BlockSpec(memory_space=pltpu.VMEM)
    return pl.pallas_call(
        params_kernel,
        out_shape=jax.ShapeDtypeStruct(params.shape, jnp.float32),
        in_specs=[vmem] * 4,
        out_specs=vmem,
        compiler_params=pltpu.CompilerParams(vmem_limit_bytes=32 * 2**20),
        cost_estimate=pl.CostEstimate(flops=60_000_000, bytes_accessed=700_000, transcendentals=0),
        name="params",
    )(parts, params, expand, rest)


def sum_pairs(step, axis):
    pairs = []
    for d in range(N_DP):
        flip = (1, 3)[(d % 2) ^ step]
        for f in range(N_FSDP):
            to = f ^ (flip if axis == "y" else 4 * flip)
            pairs.append((d * N_FSDP + f, d * N_FSDP + to))
    return pairs


def halve(x, step, axis):
    return lax.ppermute(x, BOTH, sum_pairs(step, axis))


def deal(x, axis, groups):
    return lax.all_to_all(x, axis, 0, 0, tiled=True, axis_index_groups=groups)


def share_parts(x, groups):
    return deal(jnp.broadcast_to(x, (len(groups[0]), *x.shape)), "dp", groups)


def sum_over(x, axis, groups):
    return jnp.sum(lax.all_to_all(x, axis, 0, 0, tiled=True, axis_index_groups=groups), axis=0)


def share(x, groups):
    return sum_over(jnp.broadcast_to(x, (len(groups[0]), *x.shape)), "dp", groups)


Y_GROUPS = [[z * 4 + y for y in range(4)] for z in range(4)]
PLANE_GROUPS = [[z * 8 + x * 2 + c for x in range(4)] for z in range(4) for c in range(2)]
COLUMN_GROUPS = [[z * 8 + i for z in range(4)] for i in range(8)]
PAIR_GROUPS = [
    [(lo * 8 + x * 2 + c) * N_FSDP + hi * 4 + y for c in range(2) for y in range(4)]
    for lo in range(4) for x in range(4) for hi in range(4)
]


def after(x, earlier):
    return lax.optimization_barrier((x, earlier))


def shards(grad_partials, momentum, params, kept):
    grad = grad_partials[0, 0]
    main, near, across = main_of(grad)
    across = halve(across, 0, "y")
    near = halve(near, 0, "y")
    coef, coef_sent = coef_of(kept, grad)
    state_coef, reject, expand, rest = state_of(kept, momentum)

    coef_got = halve(coef_sent, 0, "z")
    across, coef_sent, state_coef = lax.optimization_barrier((across, coef_sent, state_coef))
    last = halve(main[1] + across, 1, "y")
    coef_next = coef[1] + coef_got[1]
    coef_last = halve(coef_next, 1, "z")
    coef = coef[0] + coef_got[0] + coef_last + state_coef
    last, coef = after(last, coef)
    main = main[0] + near + last
    got = halve(main[2:], 0, "z")

    coef = sum_over(jnp.broadcast_to(coef, (2, *coef.shape)).reshape(8, OWN, COEFFS), BOTH, PAIR_GROUPS)
    last = halve(main[1] + got[1], 1, "z")
    coef = share(coef, COLUMN_GROUPS)
    coef = share_parts(coef, PLANE_GROUPS)
    new_params = new_params_of(coef, params, expand, rest)
    new_momentum = new_momentum_of(main[0] + got[0], last, momentum, reject)
    return (new_params, new_momentum)


def solution(mesh):
    placed = (
        P("dp", "fsdp", None, None, None),
        P("dp", None, "fsdp", None),
        P(None, "fsdp", None),
        P(),
    )
    return jax.shard_map(
        shards,
        mesh=mesh,
        in_specs=placed,
        out_specs=(P(None, "fsdp", None), P("dp", None, "fsdp", None)),
        check_vma=False,
    )
```
